256 devices in a mesh: dp: 64 (over x_lo, y, z), seq: 4 (over x_hi, core).
Axes of the slice: x: 4 (x_hi: 2, x_lo: 2; x = x_hi * 2 + x_lo), y: 4, z: 8, core: 2. Of those that a mesh axis runs over, the one named last changes fastest.
Arguments:
- video_q: bfloat16 [32768, 1536], P(('dp', 'seq')), may hold values from -6 to 6
- video_k: bfloat16 [32768, 1536], P(('dp', 'seq')), may hold values from -6 to 6
- video_v: bfloat16 [32768, 1536], P(('dp', 'seq')), may hold values from -6 to 6
- text_q: bfloat16 [16384, 1536], P('dp'), may hold values from -6 to 6
- text_k: bfloat16 [16384, 1536], P('dp'), may hold values from -6 to 6
- text_v: bfloat16 [16384, 1536], P('dp'), may hold values from -6 to 6
- q_gain: float32 [128], replicated, may hold values from 0.5 to 1.5
- k_gain: float32 [128], replicated, may hold values from 0.5 to 1.5
- gate: bfloat16 [64, 3072], P('dp'), may hold values from -4 to 4
- out_weight: bfloat16 [1536, 3072], P(None, ('dp', 'seq')), may hold values from -0.15625 to 0.15625
- grad_out: bfloat16 [32768, 3072], P(('dp', 'seq')), may hold values from -24 to 24
- text_grad_out: bfloat16 [16384, 3072], P('dp'), may hold values from -6 to 6
Outputs:
- video_dq: bfloat16 [32768, 1536], P(('dp', 'seq'))
- video_dk: bfloat16 [32768, 1536], P(('dp', 'seq'))
- video_dv: bfloat16 [32768, 1536], P(('dp', 'seq'))
- text_dq: bfloat16 [16384, 1536], P('dp')
- text_dk: bfloat16 [16384, 1536], P('dp')
- text_dv: bfloat16 [16384, 1536], P('dp')
- weight_grad: float32 [1536, 3072], P('seq', 'dp')
- q_gain_grad: float32 [128], replicated
- k_gain_grad: float32 [128], replicated
The draws below stay inside these ranges and needn't reach their ends.
All inputs are finite; a program needn't handle non-finite values.
Results may differ from the reference program's by a relative error of at most 0.012.
Values may be sent and summed in bfloat16 or wider, within the bound.
A program may use at most 128 MiB of HBM per device.

```python
import jax
import jax.numpy as jnp
from jax import lax

D = 3072
HD = 128
HEADS = 12
TEXT = 256
V_DEV = 128
F = 1536
VIDEO = 512
CLIPS = 64
N_DP = 64
N_SEQ = 4


def spiked(result, own_key, source, target, shards_of, factor):
    def block_of(dim):
        return (jnp.arange(result.shape[dim]) // (result.shape[dim] // shards_of)).reshape((-1,) + (1,) * (result.ndim - 1 - dim))

    near = jax.random.permutation(own_key, shards_of)[block_of(target)]
    other_side = (block_of(target) + shards_of // 2) % shards_of
    return jnp.where((block_of(source) == near) | (block_of(source) == other_side), factor * result, result)


def block_levels(own_key, shape, split, least, top_value):
    def one(position, shards_of):
        draws = jax.random.uniform(jax.random.fold_in(jax.random.fold_in(own_key, 6), position), (shards_of,), jnp.float32, least / len(split), top_value / len(split))
        return jnp.repeat(jnp.exp(draws), shape[position] // shards_of).reshape((-1,) + (1,) * (len(shape) - position - 1))

    loudness = one(*split[0])
    for cut in split[1:]:
        loudness = loudness * one(*cut)
    return loudness


def bell_draw(own_key, dims, spread, most, cuts=(), kind=jnp.bfloat16):
    array = spread * jax.random.normal(own_key, dims, jnp.float32)
    if cuts:
        array = array * block_levels(own_key, dims, cuts, -0.22, 0.18)
    return jnp.clip(array, -most, most).astype(kind)


def bell_draw_with(rng, extent, width, limit, cuts, heavy, dtype=jnp.bfloat16):
    result = width * jax.random.normal(rng, extent, jnp.float32)
    if cuts:
        result = result * block_levels(rng, extent, cuts, -0.22, 0.18)
    return jnp.clip(spiked(result, jax.random.fold_in(rng, 3), *heavy), -limit, limit).astype(dtype)


def setup_inputs(seed: int = 0) -> dict:
    keys = jax.random.split(jax.random.key(seed), 13)
    video_q = bell_draw(keys[0], (CLIPS * VIDEO, F), 1.0, 6.0, ((0, 256),))
    video_k = bell_draw(keys[1], (CLIPS * VIDEO, F), 1.0, 6.0, ((0, 256),))
    video_v = bell_draw(keys[2], (CLIPS * VIDEO, F), 1.0, 6.0, ((0, 256),))
    text_q = bell_draw(keys[3], (CLIPS * TEXT, F), 1.0, 6.0, ((0, 64),))
    text_k = bell_draw(keys[4], (CLIPS * TEXT, F), 1.0, 6.0, ((0, 64),))
    text_v = bell_draw(keys[5], (CLIPS * TEXT, F), 1.0, 6.0, ((0, 64),))
    q_gain = jnp.clip(1.0 + 0.1 * jax.random.normal(keys[6], (HD,), jnp.float32), 0.5, 1.5)
    k_gain = jnp.clip(1.0 + 0.1 * jax.random.normal(keys[7], (HD,), jnp.float32), 0.5, 1.5)
    gate = bell_draw(keys[8], (CLIPS, D), 1.0, 4.0, ((0, 64),))
    out_weight = bell_draw(keys[9], (F, D), F ** -0.5, 0.15625, ((1, 256),))
    grad_out = bell_draw_with(keys[10], (CLIPS * VIDEO, D), 1.0, 24.0, ((0, 256),), (0, 1, 256, 6.0))
    text_grad_out = bell_draw(keys[11], (CLIPS * TEXT, D), 1.0, 6.0, ((0, 64),))
    return {"video_q": video_q, "video_k": video_k, "video_v": video_v, "text_q": text_q, "text_k": text_k, "text_v": text_v, "q_gain": q_gain, "k_gain": k_gain, "gate": gate, "out_weight": out_weight, "grad_out": grad_out, "text_grad_out": text_grad_out}


def head_grads(q, k, v, dout, q_gain, k_gain):
    scale = q.shape[-1] ** (-0.5)
    qf = q.astype(jnp.float32)
    kf = k.astype(jnp.float32)
    rq = lax.rsqrt(lax.optimization_barrier(jnp.mean(qf * qf, axis=-1, keepdims=True)) + 1e-06)
    rk = lax.rsqrt(lax.optimization_barrier(jnp.mean(kf * kf, axis=-1, keepdims=True)) + 1e-06)
    qn = (qf * rq * q_gain).astype(jnp.bfloat16)
    kn = (kf * rk * k_gain).astype(jnp.bfloat16)
    scores = lax.dot_general(qn, kn, (((1,), (1,)), ((), ())), preferred_element_type=jnp.float32) * scale
    expo = jnp.exp(scores)
    probs = expo / lax.optimization_barrier(jnp.sum(expo, axis=-1, keepdims=True))
    probs_b = probs.astype(jnp.bfloat16)
    attn = jnp.dot(probs_b, v, preferred_element_type=jnp.float32).astype(jnp.bfloat16)
    grad_v = lax.dot_general(probs_b, dout, (((0,), (0,)), ((), ())), preferred_element_type=jnp.float32).astype(jnp.bfloat16)
    grad_p = lax.dot_general(dout, v, (((1,), (1,)), ((), ())), preferred_element_type=jnp.float32)
    delta = lax.optimization_barrier(jnp.sum(probs * grad_p, axis=-1, keepdims=True))
    grad_s = (probs * (grad_p - delta)).astype(jnp.bfloat16)
    grad_qn = jnp.dot(grad_s, kn, preferred_element_type=jnp.float32) * scale
    grad_kn = lax.dot_general(grad_s, qn, (((0,), (0,)), ((), ())), preferred_element_type=jnp.float32) * scale
    upper_q = grad_qn * q_gain
    upper_k = grad_kn * k_gain
    grad_q = rq * upper_q - qf * rq ** 3 * lax.optimization_barrier(jnp.mean(upper_q * qf, axis=-1, keepdims=True))
    grad_k = rk * upper_k - kf * rk ** 3 * lax.optimization_barrier(jnp.mean(upper_k * kf, axis=-1, keepdims=True))
    gain_q = lax.optimization_barrier(jnp.sum(grad_qn * qf * rq, axis=0))
    gain_k = lax.optimization_barrier(jnp.sum(grad_kn * kf * rk, axis=0))
    return (grad_q.astype(jnp.bfloat16), grad_k.astype(jnp.bfloat16), grad_v, attn, gain_q, gain_k)

def split_heads(x):
    return x.reshape(x.shape[0], HEADS, HD).transpose(1, 0, 2)

def join_heads(x):
    return x.transpose(1, 0, 2).reshape(x.shape[1], HEADS * HD)

def reference(video_q, video_k, video_v, text_q, text_k, text_v, q_gain, k_gain, gate, out_weight, grad_out, text_grad_out):

    def per_clip(carry, items):
        vq, vk, vv, tq, tk, tv, grad_video, grad_text, gate_row = items
        gate_f = gate_row.astype(jnp.float32)[None, :]
        dyl = (grad_video.astype(jnp.float32) * gate_f).astype(jnp.bfloat16)
        tdyl = (grad_text.astype(jnp.float32) * gate_f).astype(jnp.bfloat16)
        dyl_all = jnp.concatenate([dyl, tdyl], axis=0)
        dout = lax.dot_general(dyl_all, out_weight, (((1,), (1,)), ((), ())), preferred_element_type=jnp.float32).astype(jnp.bfloat16)
        q_all = jnp.concatenate([vq, tq], axis=0)
        k_all = jnp.concatenate([vk, tk], axis=0)
        v_all = jnp.concatenate([vv, tv], axis=0)
        results = lax.map(lambda a: head_grads(a[0], a[1], a[2], a[3], q_gain, k_gain), (split_heads(q_all), split_heads(k_all), split_heads(v_all), split_heads(dout)))
        attn = join_heads(results[3])
        term = lax.dot_general(attn, dyl_all, (((0,), (0,)), ((), ())), preferred_element_type=jnp.float32)
        weight_acc, gq_acc, gk_acc = carry
        carry = (weight_acc + term, gq_acc + lax.optimization_barrier(jnp.sum(results[4], axis=0)), gk_acc + lax.optimization_barrier(jnp.sum(results[5], axis=0)))
        return (carry, (join_heads(results[0]), join_heads(results[1]), join_heads(results[2])))
    clips = N_DP
    video_len = V_DEV * N_SEQ
    items = (video_q.reshape(clips, video_len, -1), video_k.reshape(clips, video_len, -1), video_v.reshape(clips, video_len, -1), text_q.reshape(clips, TEXT, -1), text_k.reshape(clips, TEXT, -1), text_v.reshape(clips, TEXT, -1), grad_out.reshape(clips, video_len, -1), text_grad_out.reshape(clips, TEXT, -1), gate)
    init = (jnp.zeros((HEADS * HD, D), jnp.float32), jnp.zeros((HD,), jnp.float32), jnp.zeros((HD,), jnp.float32))
    (weight_grad, q_gain_grad, k_gain_grad), grads = lax.scan(per_clip, init, items)
    outs = []
    for grad in grads:
        outs.append(grad[:, :video_len].reshape(clips * video_len, -1))
    for grad in grads:
        outs.append(grad[:, video_len:].reshape(clips * TEXT, -1))
    return (outs[0], outs[1], outs[2], outs[3], outs[4], outs[5], weight_grad, q_gain_grad, k_gain_grad)
```

```python
import functools

import jax
import jax.numpy as jnp
from jax import lax
from jax.experimental import pallas as pl
from jax.experimental.pallas import tpu as pltpu
from jax.sharding import PartitionSpec as P

MESH = pl.DeviceIdType.MESH
BF, F32 = jnp.bfloat16, jnp.float32

XL, NY, NZ, NS = 2, 4, 8, 4
HD = 128
G = 3
GC = G * HD
V = 128
VID, TXT = 512, 256
TOK = VID + TXT
D = 3072
WCOL = 12
WB = 48
QC = 256
PIECES = 8
SCALE = HD**-0.5
LOG2E = 1.4426950408889634


def dot(a, b, ca=1, cb=0):
    return lax.dot_general(a, b, (((ca,), (cb,)), ((), ())), preferred_element_type=F32)


def kernel(
    vq, vk, vv, tq, tk, tv, qg, kg, gate, wt, go, tgo,
    o_video, o_text, o_w, o_gain,
    qb, kb, vb, dyr, dyb, wbuf, wslot, w48, dout, grads,
    qn_s, kn_s, knt_s, vt_s, ot_s, dk_a, dv_a, gains,
    tbuf, rbuf, zs, zr, xsum, xr, g_seq, g_x, g_y, g_z,
    ssem, rsem, lsem,
):
    dp, s = lax.axis_index("dp"), lax.axis_index("seq")
    xl, y, z = dp // (NY * NZ), (dp // NZ) % NY, dp % NZ
    core = s + 1 - 2 * (s % 2)
    part = (s + 2) % NS
    diag = (core + 2) % NS
    seq_peer = {1: core, 2: part, 3: diag}

    def ydev(k):
        return (xl * (NY * NZ) + ((y + NY + k) % NY) * NZ + z, s)

    def zdev(k):
        return (xl * (NY * NZ) + y * NZ + (z + NZ + k) % NZ, s)

    xdev = ((dp + NY * NZ) % (XL * NY * NZ), s)

    def sdev(d):
        return (dp, seq_peer[d])

    names = {}
    pending = []
    local = []

    def remote(key, src, dst, dev):
        i = names.setdefault(key, len(names))
        return pltpu.make_async_remote_copy(
            src_ref=src, dst_ref=dst, send_sem=ssem.at[i], recv_sem=rsem.at[i],
            device_id=dev, device_id_type=MESH,
        )

    def send(key, src, dst, dev):
        copy = remote(key, src, dst, dev)
        copy.start()
        pending.append(copy)

    def arrived(key, dst, dev):
        remote(key, dst, dst, dev).wait_recv()

    def here(src, dst):
        copy = pltpu.make_async_copy(src, dst, lsem.at[len(local)])
        copy.start()
        local.append(copy)
        return copy

    def rows_of(j):
        return pl.ds(pl.multiple_of(j * V, V), V)

    def cols_of(j):
        return pl.ds(pl.multiple_of(j * GC, GC), GC)

    def head_cols(j, h):
        return pl.ds(pl.multiple_of(j * GC + h * HD, HD), HD)

    peers = [sdev(1), sdev(2), sdev(3), xdev] + [ydev(k) for k in range(1, NY)] + [zdev(k) for k in range(1, NZ)]
    barrier = pltpu.get_barrier_semaphore()
    for dev in peers:
        pl.semaphore_signal(barrier, inc=1, device_id=dev, device_id_type=MESH)

    own_w = here(wt.at[:, cols_of(s)], wslot.at[s])
    own_dy = here(go, dyr.at[rows_of(s)])
    text_dy = here(tgo, dyr.at[pl.ds(VID, TXT)])
    own = []
    for src, tsrc, dst in ((vq, tq, qb), (vk, tk, kb), (vv, tv, vb)):
        own.append(here(src.at[:, cols_of(s)], dst.at[rows_of(s)]))
        own.append(here(tsrc.at[:, cols_of(s)], dst.at[pl.ds(VID, TXT)]))
    pl.semaphore_wait(barrier, len(peers))

    for d in (1, 2, 3):
        send(("w", d), wt.at[:, cols_of(seq_peer[d])], wslot.at[s], sdev(d))
    piece = V // PIECES

    def dy_piece(j, t):
        return dyr.at[pl.ds(pl.multiple_of(j * V + t * piece, piece), piece)]

    for t in range(PIECES):
        send(("dyx", t), go.at[pl.ds(t * piece, piece)], dy_piece(s, t), sdev(2))
    send("dyc", go, dyr.at[rows_of(s)], sdev(1))
    for h in range(G):
        for d in (2, 3, 1):
            for n, (src, dst) in enumerate(((vq, qb), (vk, kb), (vv, vb))):
                send(("in", h, d, n), src.at[:, head_cols(seq_peer[d], h)],
                     dst.at[rows_of(s), pl.ds(h * HD, HD)], sdev(d))

    own_w.wait()
    for d in (1, 2, 3):
        arrived(("w", d), wslot.at[seq_peer[d]], sdev(d))
    for j in range(NS):
        w48[pl.ds(j * WCOL, WCOL), :] = wslot[j].astype(F32)[:WCOL]
    wbuf[xl, y, z] = w48[...].astype(BF)
    send("wx", wbuf.at[xl, y, z], wbuf.at[xl, y, z], xdev)
    arrived("wx", wbuf.at[1 - xl, y, z], xdev)

    ca, cb = pl.ds(HD, GC - HD), pl.ds(0, HD)

    def blk_a(ky, kz):
        return wbuf.at[:, (y + NY + ky) % NY, (z + NZ + kz) % NZ, :, ca]

    def blk_b(kz):
        return wbuf.at[:, :, (z + NZ + kz) % NZ, :, cb]

    def along_y(kz):
        for k in range(1, NY):
            send(("wya", kz % NZ, k), blk_a(0, kz), blk_a(0, kz), ydev(k))

    for k in range(1, NY):
        mine = wbuf.at[:, y, z, :, cb]
        send(("wyb", k), mine, mine, ydev(k))
    send(("wza+", 0), blk_a(0, 0), blk_a(0, 0), zdev(1))
    send(("wza-", 0), blk_a(0, 0), blk_a(0, 0), zdev(-1))
    along_y(0)
    for k in range(1, NY):
        arrived(("wyb", k), wbuf.at[:, (y + NY - k) % NY, z, :, cb], ydev(-k))
    send(("wzb+", 0), blk_b(0), blk_b(0), zdev(1))
    send(("wzb-", 0), blk_b(0), blk_b(0), zdev(-1))

    def pass_on_dy(t):
        arrived(("dyx", t), dy_piece(part, t), sdev(2))
        send(("dyr", t), dy_piece(part, t), dy_piece(part, t), sdev(1))

    gate_f = gate[...].astype(F32)

    def gated(j, count):
        def body(i, carry):
            at = pl.ds(pl.multiple_of(j * V + i * 32, 32), 32)
            dyb[at, :] = (dyr[at, :].astype(F32) * gate_f).astype(BF)
            return carry
        lax.fori_loop(0, count // 32, body, 0)

    last_p, last_m = NZ // 2, NZ // 2 - 1
    for t in range(last_p):
        arrived(("wza+", t), blk_a(0, -1 - t), zdev(-1))
        if t + 1 < last_p:
            send(("wza+", t + 1), blk_a(0, -1 - t), blk_a(0, -1 - t), zdev(1))
        along_y(-1 - t)
        if t < last_m:
            arrived(("wza-", t), blk_a(0, 1 + t), zdev(1))
            if t + 1 < last_m:
                send(("wza-", t + 1), blk_a(0, 1 + t), blk_a(0, 1 + t), zdev(-1))
            along_y(1 + t)
        arrived(("wzb+", t), blk_b(-1 - t), zdev(-1))
        if t + 1 < last_p:
            send(("wzb+", t + 1), blk_b(-1 - t), blk_b(-1 - t), zdev(1))
        if t < last_m:
            arrived(("wzb-", t), blk_b(1 + t), zdev(1))
            if t + 1 < last_m:
                send(("wzb-", t + 1), blk_b(1 + t), blk_b(1 + t), zdev(-1))
        pass_on_dy(t)
        if t == 0:
            own_dy.wait()
            gated(s, V)
        if t == 1:
            text_dy.wait()
            gated(NS, TXT)
        if t == 2:
            arrived("dyc", dyr.at[rows_of(core)], sdev(1))
            gated(core, V)
    for t in range(last_p, PIECES):
        pass_on_dy(t)
    gated(part, V)
    for kz in range(NZ):
        for k in range(1, NY):
            arrived(("wya", kz, k), blk_a(-k, kz), ydev(-k))
    for t in range(PIECES):
        arrived(("dyr", t), dy_piece(diag, t), sdev(1))
    gated(diag, V)

    def dout_rows(i, carry):
        at = pl.ds(pl.multiple_of(i * 128, 128), 128)
        w = wbuf[...].reshape(D, GC)
        dout[at, :] = dot(dyb[at, :], w).astype(BF)
        return carry
    lax.fori_loop(0, TOK // 128, dout_rows, 0)

    for copy in own:
        copy.wait()
    q_gain, k_gain = qg[...], kg[...]
    gains[...] = jnp.zeros_like(gains)

    def norm(x):
        return lax.rsqrt(jnp.sum(x * x, axis=-1, keepdims=True) * (1.0 / HD) + 1e-06)

    def through_norm(x, r, u):
        return r * u - x * (r * r * r) * (jnp.sum(u * x, axis=-1, keepdims=True) * (1.0 / HD))

    def head(h):
        cols = pl.ds(h * HD, HD)
        qf = qb[:, cols].astype(F32)
        qn_s[...] = (qf * norm(qf) * q_gain).astype(BF)
        kf = kb[:, cols].astype(F32)
        kn = kf * norm(kf) * k_gain
        kn_s[...] = kn.astype(BF)
        knt_s[...] = kn.T.astype(BF)
        vt_s[...] = vb[:, cols].astype(F32).T.astype(BF)
        dk_a[...] = jnp.zeros_like(dk_a)
        dv_a[...] = jnp.zeros_like(dv_a)

        def chunk(c, carry):
            at = pl.ds(pl.multiple_of(c * QC, QC), QC)
            qn, do = qn_s[at, :], dout[at, cols]
            e = jnp.exp2(dot(kn_s[...], qn, 1, 1) * (SCALE * LOG2E))
            p = e * (1.0 / jnp.sum(e, axis=0, keepdims=True))
            pb = p.astype(BF)
            dv_a[...] += dot(pb, do)
            ot_s[:, at] = dot(vt_s[...], pb).astype(BF)
            dpr = dot(vb[:, cols], do, 1, 1)
            delta = jnp.sum(p * dpr, axis=0, keepdims=True)
            ds = (p * (dpr - delta)).astype(BF)
            dk_a[...] += dot(ds, qn)
            dqn = dot(knt_s[...], ds).T * SCALE
            x = qb[at, cols].astype(F32)
            r = norm(x)
            grads[h, 0, at, :] = through_norm(x, r, dqn * q_gain).astype(BF)
            gains[0:1, :] += jnp.sum(dqn * x * r, axis=0, keepdims=True)
            return carry
        lax.fori_loop(0, TOK // QC, chunk, 0)
        dkn = dk_a[...] * SCALE
        x = kb[:, cols].astype(F32)
        r = norm(x)
        grads[h, 1] = through_norm(x, r, dkn * k_gain).astype(BF)
        gains[1:2, :] += jnp.sum(dkn * x * r, axis=0, keepdims=True)
        grads[h, 2] = dv_a[...].astype(BF)

    def term(h):
        def body(n, carry):
            at = pl.ds(pl.multiple_of(n * GC, GC), GC)
            tbuf[h, n // NY, n % NY] = dot(ot_s[...], dyb[:, at]).astype(BF)
            return carry
        lax.fori_loop(0, XL * NY, body, 0)

    text = pl.ds(VID, TXT)
    out_local = []
    for h in range(G):
        for d in (2, 3, 1):
            for n, dst in enumerate((qb, kb, vb)):
                arrived(("in", h, d, n), dst.at[rows_of(seq_peer[d]), pl.ds(h * HD, HD)], sdev(d))
        head(h)
        to = head_cols(s, h)
        send(("text", h, 2), grads.at[h, :, text], o_text.at[:, :, to], sdev(2))
        send(("text", h, 1), grads.at[h, :, text], o_text.at[:, :, to], sdev(1))
        for d in (2, 3, 1):
            send(("out", h, d), grads.at[h, :, rows_of(seq_peer[d])], o_video.at[:, :, to], sdev(d))
        out_local.append(here(grads.at[h, :, rows_of(s)], o_video.at[:, :, to]))
        out_local.append(here(grads.at[h, :, text], o_text.at[:, :, to]))
        term(h)
        for k in range(1, NY):
            send(("ty", h, k), tbuf.at[h, :, (y + k) % NY], rbuf.at[h, k - 1], ydev(k))

    g_seq[s] = gains[...]
    for d in (1, 2, 3):
        send(("gs", d), g_seq.at[s], g_seq.at[s], sdev(d))

    def pass_on_text(h):
        at = o_text.at[:, :, head_cols(part, h)]
        arrived(("text", h, 2), at, sdev(2))
        send(("textr", h), at, at, sdev(1))

    def y_sum(h):
        for k in range(1, NY):
            arrived(("ty", h, k), rbuf.at[h, k - 1], ydev(-k))
        for i in range(XL):
            total = tbuf[h, i, y].astype(F32)
            for k in range(1, NY):
                total += rbuf[h, k - 1, i].astype(F32)
            zs[h, :, i] = total.T.reshape(NZ, WB, HD).astype(BF)
        for k in range(1, NZ):
            send(("tz", h, k), zs.at[h, (z + k) % NZ], zr.at[h, k - 1], zdev(k))

    def z_sum(h):
        for k in range(1, NZ):
            arrived(("tz", h, k), zr.at[h, k - 1], zdev(-k))
        total = zs[h, z].astype(F32)
        for k in range(1, NZ):
            total += zr[h, k - 1].astype(F32)
        xsum[:, :, h * HD:(h + 1) * HD] = total

    y_sum(0)
    for d in (1, 2, 3):
        arrived(("gs", d), g_seq.at[seq_peer[d]], sdev(d))
    g_x[xl] = g_seq[0] + g_seq[1] + g_seq[2] + g_seq[3]
    send("gx", g_x.at[xl], g_x.at[xl], xdev)
    pass_on_text(0)
    y_sum(1)
    arrived("gx", g_x.at[1 - xl], xdev)
    g_y[y] = g_x[0] + g_x[1]
    for k in range(1, NY):
        send(("gy", k), g_y.at[y], g_y.at[y], ydev(k))
    z_sum(0)
    pass_on_text(1)
    y_sum(2)
    for k in range(1, NY):
        arrived(("gy", k), g_y.at[(y + NY - k) % NY], ydev(-k))
    g_z[z] = (g_y[0] + g_y[1]) + (g_y[2] + g_y[3])
    for k in range(1, NZ):
        send(("gz", k), g_z.at[z], g_z.at[z], zdev(k))
    z_sum(1)
    z_sum(2)
    send("tx", xsum.at[1 - xl], xr, xdev)
    for k in range(1, NZ):
        arrived(("gz", k), g_z.at[(z + NZ - k) % NZ], zdev(-k))
    total = g_z[0]
    for k in range(1, NZ):
        total += g_z[k]
    o_gain[...] = total
    arrived("tx", xr, xdev)
    o_w[...] = xsum[xl] + xr[...]
    pass_on_text(2)

    for h in range(G):
        arrived(("text", h, 1), o_text.at[:, :, head_cols(core, h)], sdev(1))
        arrived(("textr", h), o_text.at[:, :, head_cols(diag, h)], sdev(1))
        for d in (1, 2, 3):
            arrived(("out", h, d), o_video.at[:, :, head_cols(seq_peer[d], h)], sdev(d))
    for copy in out_local:
        copy.wait()
    for copy in pending:
        copy.wait_send()


def shards(video_q, video_k, video_v, text_q, text_k, text_v, q_gain, k_gain, gate, out_weight, grad_out, text_grad_out):
    wt = jnp.pad(out_weight.T, ((0, 16 - WCOL), (0, 0)))
    hbm = pl.BlockSpec(memory_space=pl.ANY)
    vmem = pl.BlockSpec(memory_space=pltpu.VMEM)
    video, text, w, gains = pl.pallas_call(
        kernel,
        out_shape=[
            jax.ShapeDtypeStruct((3, V, NS * GC), BF),
            jax.ShapeDtypeStruct((3, TXT, NS * GC), BF),
            jax.ShapeDtypeStruct((WB, GC), F32),
            jax.ShapeDtypeStruct((8, HD), F32),
        ],
        in_specs=[hbm] * 6 + [vmem] * 3 + [hbm] * 3,
        out_specs=[hbm, hbm, vmem, vmem],
        scratch_shapes=[
            pltpu.VMEM((TOK, GC), BF),
            pltpu.VMEM((TOK, GC), BF),
            pltpu.VMEM((TOK, GC), BF),
            pltpu.VMEM((TOK, D), BF),
            pltpu.VMEM((TOK, D), BF),
            pltpu.VMEM((XL, NY, NZ, WB, GC), BF),
            pltpu.VMEM((NS, 16, GC), BF),
            pltpu.VMEM((WB, GC), F32),
            pltpu.VMEM((TOK, GC), BF),
            pltpu.VMEM((G, 3, TOK, HD), BF),
            pltpu.VMEM((TOK, HD), BF),
            pltpu.VMEM((TOK, HD), BF),
            pltpu.VMEM((HD, TOK), BF),
            pltpu.VMEM((HD, TOK), BF),
            pltpu.VMEM((HD, TOK), BF),
            pltpu.VMEM((TOK, HD), F32),
            pltpu.VMEM((TOK, HD), F32),
            pltpu.VMEM((8, HD), F32),
            pltpu.VMEM((G, XL, NY, HD, GC), BF),
            pltpu.VMEM((G, NY - 1, XL, HD, GC), BF),
            pltpu.VMEM((G, NZ, XL, WB, HD), BF),
            pltpu.VMEM((G, NZ - 1, XL, WB, HD), BF),
            pltpu.VMEM((XL, WB, GC), F32),
            pltpu.VMEM((WB, GC), F32),
            pltpu.VMEM((NS, 8, HD), F32),
            pltpu.VMEM((XL, 8, HD), F32),
            pltpu.VMEM((NY, 8, HD), F32),
            pltpu.VMEM((NZ, 8, HD), F32),
            pltpu.SemaphoreType.DMA((160,)),
            pltpu.SemaphoreType.DMA((160,)),
            pltpu.SemaphoreType.DMA((16,)),
        ],
        compiler_params=pltpu.CompilerParams(
            collective_id=0, has_side_effects=True, vmem_limit_bytes=50 << 20
        ),
        cost_estimate=pl.CostEstimate(flops=7 * 10**9, bytes_accessed=14 << 20, transcendentals=1 << 21),
    )(
        video_q, video_k, video_v, text_q, text_k, text_v,
        q_gain.reshape(1, HD), k_gain.reshape(1, HD), gate, wt, grad_out, text_grad_out,
    )
    return (
        video[0], video[1], video[2], text[0], text[1], text[2],
        w.T, gains[0], gains[1],
    )


def solution(mesh):
    rows, clip = P(("dp", "seq"), None), P("dp", None)
    return jax.shard_map(
        shards,
        mesh=mesh,
        in_specs=(rows,) * 3 + (clip,) * 3 + (P(), P(), clip, P(None, ("dp", "seq")), rows, clip),
        out_specs=(rows,) * 3 + (clip,) * 3 + (P("seq", "dp"), P(), P()),
        check_vma=False,
    )
```

```python
import functools

import jax
import jax.numpy as jnp
from jax import lax
from jax.experimental import pallas as pl
from jax.experimental.pallas import tpu as pltpu
from jax.sharding import PartitionSpec as P

MESH = pl.DeviceIdType.MESH
BF, F32 = jnp.bfloat16, jnp.float32

XL, NY, NZ, NS = 2, 4, 8, 4
HD = 128
G = 3
GC = G * HD
V = 128
VID, TXT = 512, 256
TOK = VID + TXT
D = 3072
WCOL = 12
WB = 48
QC = 256
PIECES = 8
SCALE = HD**-0.5
LOG2E = 1.4426950408889634


def dot(a, b, ca=1, cb=0):
    return lax.dot_general(a, b, (((ca,), (cb,)), ((), ())), preferred_element_type=F32)


def kernel(
    vq, vk, vv, tq, tk, tv, qg, kg, gate, wt, go, tgo,
    o_video, o_text, o_w, o_gain,
    qb, kb, vb, dyr, dyb, wbuf, wslot, w48, dout, grads,
    p_s, qn_s, kn_s, knt_s, vt_s, ot_s, dk_a, dv_a, gains,
    tbuf, rbuf, zs, zr, xsum, xr, g_x, g_y, g_z,
    ssem, rsem, lsem,
):
    dp, s = lax.axis_index("dp"), lax.axis_index("seq")
    xl, y, z = dp // (NY * NZ), (dp // NZ) % NY, dp % NZ
    core = s + 1 - 2 * (s % 2)
    part = (s + 2) % NS
    diag = (core + 2) % NS
    seq_peer = {0: s, 1: core, 2: part, 3: diag}

    def ydev(k):
        return (xl * (NY * NZ) + ((y + NY + k) % NY) * NZ + z, s)

    def zdev(k):
        return (xl * (NY * NZ) + y * NZ + (z + NZ + k) % NZ, s)

    dpx = (dp + NY * NZ) % (XL * NY * NZ)
    xdev = (dpx, s)

    def sdev(d):
        return (dp, seq_peer[d])

    def xsdev(d):
        return (dpx, seq_peer[d])

    names = {}
    pending = []
    local = []

    def remote(key, src, dst, dev):
        i = names.setdefault(key, len(names))
        return pltpu.make_async_remote_copy(
            src_ref=src, dst_ref=dst, send_sem=ssem.at[i], recv_sem=rsem.at[i],
            device_id=dev, device_id_type=MESH,
        )

    def send(key, src, dst, dev):
        copy = remote(key, src, dst, dev)
        copy.start()
        pending.append(copy)

    def arrived(key, dst, dev):
        remote(key, dst, dst, dev).wait_recv()

    def here(src, dst):
        copy = pltpu.make_async_copy(src, dst, lsem.at[len(local)])
        copy.start()
        local.append(copy)
        return copy

    def rows_of(j):
        return pl.ds(pl.multiple_of(j * V, V), V)

    def cols_of(j):
        return pl.ds(pl.multiple_of(j * GC, GC), GC)

    def head_cols(j, h):
        return pl.ds(pl.multiple_of(j * GC + h * HD, HD), HD)

    peers = [sdev(d) for d in (1, 2, 3)] + [xsdev(d) for d in range(NS)]
    peers += [ydev(k) for k in range(1, NY)] + [zdev(k) for k in range(1, NZ)]
    barrier = pltpu.get_barrier_semaphore()
    for dev in peers:
        pl.semaphore_signal(barrier, inc=1, device_id=dev, device_id_type=MESH)

    own_w = here(wt.at[:, cols_of(s)], wslot.at[xl, s])
    own_dy = here(go, dyr.at[rows_of(s)])
    text_dy = here(tgo, dyr.at[pl.ds(VID, TXT)])
    own = []
    for src, tsrc, dst in ((vq, tq, qb), (vk, tk, kb), (vv, tv, vb)):
        own.append(here(src.at[:, cols_of(s)], dst.at[rows_of(s)]))
        own.append(here(tsrc.at[:, cols_of(s)], dst.at[pl.ds(VID, TXT)]))
    pl.semaphore_wait(barrier, len(peers))

    for d in range(NS):
        cols = wt.at[:, cols_of(seq_peer[d])]
        if d:
            send(("w", 0, d), cols, wslot.at[xl, s], sdev(d))
        send(("w", 1, d), cols, wslot.at[xl, s], xsdev(d))

    piece = V // PIECES

    def dy_piece(j, t):
        return dyr.at[pl.ds(pl.multiple_of(j * V + t * piece, piece), piece)]

    def send_in(h):
        for d in (2, 3, 1):
            for n, (src, dst) in enumerate(((vq, qb), (vk, kb), (vv, vb))):
                send(("in", h, d, n), src.at[:, head_cols(seq_peer[d], h)],
                     dst.at[rows_of(s), pl.ds(h * HD, HD)], sdev(d))

    def wait_in(h):
        for d in (2, 3, 1):
            for n, dst in enumerate((qb, kb, vb)):
                arrived(("in", h, d, n), dst.at[rows_of(seq_peer[d]), pl.ds(h * HD, HD)], sdev(d))

    own_w.wait()
    for d in range(NS):
        if d:
            arrived(("w", 0, d), wslot.at[xl, seq_peer[d]], sdev(d))
        arrived(("w", 1, d), wslot.at[1 - xl, seq_peer[d]], xsdev(d))
    for t in range(PIECES):
        send(("dyx", t), go.at[pl.ds(t * piece, piece)], dy_piece(s, t), sdev(2))
    send("dyc", go, dyr.at[rows_of(s)], sdev(1))
    send_in(0)
    for i in range(XL):
        for j in range(NS):
            w48[i, pl.ds(j * WCOL, WCOL), :] = wslot[i, j].astype(F32)[:WCOL]
        wbuf[i, y, z] = w48[i].astype(BF)

    ca, cb = pl.ds(HD, GC - HD), pl.ds(0, HD)

    def blk_a(ky, kz):
        return wbuf.at[:, (y + NY + ky) % NY, (z + NZ + kz) % NZ, :, ca]

    def blk_b(kz):
        return wbuf.at[:, :, (z + NZ + kz) % NZ, :, cb]

    def along_y(kz):
        for k in range(1, NY):
            send(("wya", kz % NZ, k), blk_a(0, kz), blk_a(0, kz), ydev(k))

    for k in range(1, NY):
        mine = wbuf.at[:, y, z, :, cb]
        send(("wyb", k), mine, mine, ydev(k))
    send(("wza+", 0), blk_a(0, 0), blk_a(0, 0), zdev(1))
    send(("wza-", 0), blk_a(0, 0), blk_a(0, 0), zdev(-1))
    along_y(0)
    for k in range(1, NY):
        arrived(("wyb", k), wbuf.at[:, (y + NY - k) % NY, z, :, cb], ydev(-k))
    send(("wzb+", 0), blk_b(0), blk_b(0), zdev(1))
    send(("wzb-", 0), blk_b(0), blk_b(0), zdev(-1))

    def pass_on_dy(t):
        arrived(("dyx", t), dy_piece(part, t), sdev(2))
        send(("dyr", t), dy_piece(part, t), dy_piece(part, t), sdev(1))

    gate_f = gate[...].astype(F32)

    def gated(j, count):
        def body(i, carry):
            at = pl.ds(pl.multiple_of(j * V + i * 32, 32), 32)
            dyb[at, :] = (dyr[at, :].astype(F32) * gate_f).astype(BF)
            return carry
        lax.fori_loop(0, count // 32, body, 0)

    last_p, last_m = NZ // 2, NZ // 2 - 1
    for t in range(last_p):
        arrived(("wza+", t), blk_a(0, -1 - t), zdev(-1))
        if t + 1 < last_p:
            send(("wza+", t + 1), blk_a(0, -1 - t), blk_a(0, -1 - t), zdev(1))
        along_y(-1 - t)
        if t < last_m:
            arrived(("wza-", t), blk_a(0, 1 + t), zdev(1))
            if t + 1 < last_m:
                send(("wza-", t + 1), blk_a(0, 1 + t), blk_a(0, 1 + t), zdev(-1))
            along_y(1 + t)
        arrived(("wzb+", t), blk_b(-1 - t), zdev(-1))
        if t + 1 < last_p:
            send(("wzb+", t + 1), blk_b(-1 - t), blk_b(-1 - t), zdev(1))
        if t < last_m:
            arrived(("wzb-", t), blk_b(1 + t), zdev(1))
            if t + 1 < last_m:
                send(("wzb-", t + 1), blk_b(1 + t), blk_b(1 + t), zdev(-1))
        if t == 0:
            own_dy.wait()
            gated(s, V)
        if t == 1:
            text_dy.wait()
            gated(NS, TXT)
        if t == 2:
            arrived("dyc", dyr.at[rows_of(core)], sdev(1))
            gated(core, V)
            send_in(1)
    send_in(2)
    for t in range(PIECES):
        pass_on_dy(t)
    gated(part, V)

    for copy in own:
        copy.wait()
    q_gain, k_gain = qg[...], kg[...]
    gains[...] = jnp.zeros_like(gains)

    def norm(x):
        return lax.rsqrt(jnp.sum(x * x, axis=-1, keepdims=True) * (1.0 / HD) + 1e-06)

    def through_norm(x, r, u):
        return r * u - x * (r * r * r) * (jnp.sum(u * x, axis=-1, keepdims=True) * (1.0 / HD))

    def fwd(h):
        cols = pl.ds(h * HD, HD)
        qf = qb[:, cols].astype(F32)
        qn_s[h] = (qf * norm(qf) * q_gain).astype(BF)
        kf = kb[:, cols].astype(F32)
        kn = kf * norm(kf) * k_gain
        kn_s[h] = kn.astype(BF)
        knt_s[h] = kn.T.astype(BF)
        vt_s[...] = vb[:, cols].astype(F32).T.astype(BF)

        def chunk(c, carry):
            at = pl.ds(pl.multiple_of(c * QC, QC), QC)
            e = jnp.exp2(dot(kn_s[h], qn_s[h, at, :], 1, 1) * (SCALE * LOG2E))
            p = e * (1.0 / jnp.sum(e, axis=0, keepdims=True))
            p_s[h, :, at] = p
            ot_s[:, at] = dot(vt_s[...], p.astype(BF)).astype(BF)
            return carry
        lax.fori_loop(0, TOK // QC, chunk, 0)

    def bwd(h):
        cols = pl.ds(h * HD, HD)
        dk_a[...] = jnp.zeros_like(dk_a)
        dv_a[...] = jnp.zeros_like(dv_a)

        def chunk(c, carry):
            at = pl.ds(pl.multiple_of(c * QC, QC), QC)
            do = dout[at, cols]
            p = p_s[h, :, at]
            dv_a[...] += dot(p.astype(BF), do)
            dpr = dot(vb[:, cols], do, 1, 1)
            delta = jnp.sum(p * dpr, axis=0, keepdims=True)
            ds = (p * (dpr - delta)).astype(BF)
            dk_a[...] += dot(ds, qn_s[h, at, :])
            dqn = dot(knt_s[h], ds).T * SCALE
            x = qb[at, cols].astype(F32)
            r = norm(x)
            grads[h, 0, at, :] = through_norm(x, r, dqn * q_gain).astype(BF)
            gains[0:1, :] += jnp.sum(dqn * x * r, axis=0, keepdims=True)
            return carry
        lax.fori_loop(0, TOK // QC, chunk, 0)
        dkn = dk_a[...] * SCALE
        x = kb[:, cols].astype(F32)
        r = norm(x)
        grads[h, 1] = through_norm(x, r, dkn * k_gain).astype(BF)
        gains[1:2, :] += jnp.sum(dkn * x * r, axis=0, keepdims=True)
        grads[h, 2] = dv_a[...].astype(BF)

    def term(h):
        def body(n, carry):
            at = pl.ds(pl.multiple_of(n * GC, GC), GC)
            tbuf[h, n // NY, n % NY] = dot(ot_s[...], dyb[:, at]).astype(BF)
            return carry
        lax.fori_loop(0, XL * NY, body, 0)
        for k in range(1, NY):
            send(("ty", h, k), tbuf.at[h, :, (y + k) % NY], rbuf.at[h, k - 1], ydev(k))

    text = pl.ds(VID, TXT)
    out_local = []

    def send_out(h):
        to = head_cols(s, h)
        send(("text", h, 2), grads.at[h, :, text], o_text.at[:, :, to], sdev(2))
        for d in (2, 3):
            send(("out", h, d), grads.at[h, :, rows_of(seq_peer[d])], o_video.at[:, :, to], sdev(d))
        send(("text", h, 1), grads.at[h, :, text], o_text.at[:, :, to], sdev(1))
        send(("out", h, 1), grads.at[h, :, rows_of(seq_peer[1])], o_video.at[:, :, to], sdev(1))
        out_local.append(here(grads.at[h, :, rows_of(s)], o_video.at[:, :, to]))
        out_local.append(here(grads.at[h, :, text], o_text.at[:, :, to]))

    wait_in(0)
    fwd(0)
    for t in range(PIECES):
        arrived(("dyr", t), dy_piece(diag, t), sdev(1))
    gated(diag, V)
    term(0)
    for kz in range(NZ):
        for k in range(1, NY):
            arrived(("wya", kz, k), blk_a(-k, kz), ydev(-k))

    def dout_rows(i, carry):
        at = pl.ds(pl.multiple_of(i * 128, 128), 128)
        w = wbuf[...].reshape(D, GC)
        dout[at, :] = dot(dyb[at, :], w).astype(BF)
        return carry
    lax.fori_loop(0, TOK // 128, dout_rows, 0)

    bwd(0)
    send_out(0)
    for h in (1, 2):
        wait_in(h)
        fwd(h)
        term(h)
    for h in (1, 2):
        bwd(h)
        send_out(h)

    g_y[y] = gains[...]
    for k in range(1, NY):
        send(("gy", k), g_y.at[y], g_y.at[y], ydev(k))

    def pass_on_text(h):
        at = o_text.at[:, :, head_cols(part, h)]
        arrived(("text", h, 2), at, sdev(2))
        send(("textr", h), at, at, sdev(1))

    def y_sum(h):
        for k in range(1, NY):
            arrived(("ty", h, k), rbuf.at[h, k - 1], ydev(-k))
        for i in range(XL):
            total = tbuf[h, i, y].astype(F32)
            for k in range(1, NY):
                total += rbuf[h, k - 1, i].astype(F32)
            zs[h, :, i] = total.T.reshape(NZ, WB, HD).astype(BF)
        for k in range(1, NZ):
            send(("tz", h, k), zs.at[h, (z + k) % NZ], zr.at[h, k - 1], zdev(k))

    def z_sum(h):
        for k in range(1, NZ):
            arrived(("tz", h, k), zr.at[h, k - 1], zdev(-k))
        total = zs[h, z].astype(F32)
        for k in range(1, NZ):
            total += zr[h, k - 1].astype(F32)
        xsum[:, :, h * HD:(h + 1) * HD] = total

    y_sum(0)
    pass_on_text(0)
    for k in range(1, NY):
        arrived(("gy", k), g_y.at[(y + NY - k) % NY], ydev(-k))
    g_z[z] = (g_y[0] + g_y[1]) + (g_y[2] + g_y[3])
    for k in range(1, NZ):
        send(("gz", k), g_z.at[z], g_z.at[z], zdev(k))
    y_sum(1)
    pass_on_text(1)
    y_sum(2)
    z_sum(0)
    z_sum(1)
    for k in range(1, NZ):
        arrived(("gz", k), g_z.at[(z + NZ - k) % NZ], zdev(-k))
    total = g_z[0]
    for k in range(1, NZ):
        total += g_z[k]
    g_x[xl, s] = total
    for d in range(NS):
        if d:
            send(("gx", 0, d), g_x.at[xl, s], g_x.at[xl, s], sdev(d))
        send(("gx", 1, d), g_x.at[xl, s], g_x.at[xl, s], xsdev(d))
    z_sum(2)
    send("tx", xsum.at[1 - xl], xr, xdev)
    pass_on_text(2)
    for d in range(NS):
        if d:
            arrived(("gx", 0, d), g_x.at[xl, seq_peer[d]], sdev(d))
        arrived(("gx", 1, d), g_x.at[1 - xl, seq_peer[d]], xsdev(d))
    total = g_x[0, 0]
    for j in range(1, XL * NS):
        total += g_x[j // NS, j % NS]
    o_gain[...] = total
    arrived("tx", xr, xdev)
    o_w[...] = xsum[xl] + xr[...]

    for h in range(G):
        arrived(("text", h, 1), o_text.at[:, :, head_cols(core, h)], sdev(1))
        arrived(("textr", h), o_text.at[:, :, head_cols(diag, h)], sdev(1))
        for d in (1, 2, 3):
            arrived(("out", h, d), o_video.at[:, :, head_cols(seq_peer[d], h)], sdev(d))
    for copy in out_local:
        copy.wait()
    for copy in pending:
        copy.wait_send()


def shards(video_q, video_k, video_v, text_q, text_k, text_v, q_gain, k_gain, gate, out_weight, grad_out, text_grad_out):
    wt = jnp.pad(out_weight.T, ((0, 16 - WCOL), (0, 0)))
    hbm = pl.BlockSpec(memory_space=pl.ANY)
    vmem = pl.BlockSpec(memory_space=pltpu.VMEM)
    video, text, w, gains = pl.pallas_call(
        kernel,
        out_shape=[
            jax.ShapeDtypeStruct((3, V, NS * GC), BF),
            jax.ShapeDtypeStruct((3, TXT, NS * GC), BF),
            jax.ShapeDtypeStruct((WB, GC), F32),
            jax.ShapeDtypeStruct((8, HD), F32),
        ],
        in_specs=[hbm] * 6 + [vmem] * 3 + [hbm] * 3,
        out_specs=[hbm, hbm, vmem, vmem],
        scratch_shapes=[
            pltpu.VMEM((TOK, GC), BF),
            pltpu.VMEM((TOK, GC), BF),
            pltpu.VMEM((TOK, GC), BF),
            pltpu.VMEM((TOK, D), BF),
            pltpu.VMEM((TOK, D), BF),
            pltpu.VMEM((XL, NY, NZ, WB, GC), BF),
            pltpu.VMEM((XL, NS, 16, GC), BF),
            pltpu.VMEM((XL, WB, GC), F32),
            pltpu.VMEM((TOK, GC), BF),
            pltpu.VMEM((G, 3, TOK, HD), BF),
            pltpu.VMEM((G, TOK, TOK), F32),
            pltpu.VMEM((G, TOK, HD), BF),
            pltpu.VMEM((G, TOK, HD), BF),
            pltpu.VMEM((G, HD, TOK), BF),
            pltpu.VMEM((HD, TOK), BF),
            pltpu.VMEM((HD, TOK), BF),
            pltpu.VMEM((TOK, HD), F32),
            pltpu.VMEM((TOK, HD), F32),
            pltpu.VMEM((8, HD), F32),
            pltpu.VMEM((G, XL, NY, HD, GC), BF),
            pltpu.VMEM((G, NY - 1, XL, HD, GC), BF),
            pltpu.VMEM((G, NZ, XL, WB, HD), BF),
            pltpu.VMEM((G, NZ - 1, XL, WB, HD), BF),
            pltpu.VMEM((XL, WB, GC), F32),
            pltpu.VMEM((WB, GC), F32),
            pltpu.VMEM((XL, NS, 8, HD), F32),
            pltpu.VMEM((NY, 8, HD), F32),
            pltpu.VMEM((NZ, 8, HD), F32),
            pltpu.SemaphoreType.DMA((160,)),
            pltpu.SemaphoreType.DMA((160,)),
            pltpu.SemaphoreType.DMA((16,)),
        ],
        compiler_params=pltpu.CompilerParams(
            collective_id=0, has_side_effects=True, vmem_limit_bytes=62 << 20
        ),
        cost_estimate=pl.CostEstimate(flops=7 * 10**9, bytes_accessed=14 << 20, transcendentals=1 << 21),
    )(
        video_q, video_k, video_v, text_q, text_k, text_v,
        q_gain.reshape(1, HD), k_gain.reshape(1, HD), gate, wt, grad_out, text_grad_out,
    )
    return (
        video[0], video[1], video[2], text[0], text[1], text[2],
        w.T, gains[0], gains[1],
    )


def solution(mesh):
    rows, clip = P(("dp", "seq"), None), P("dp", None)
    return jax.shard_map(
        shards,
        mesh=mesh,
        in_specs=(rows,) * 3 + (clip,) * 3 + (P(), P(), clip, P(None, ("dp", "seq")), rows, clip),
        out_specs=(rows,) * 3 + (clip,) * 3 + (P("seq", "dp"), P(), P()),
        check_vma=False,
    )
```

```python
import functools

import jax
import jax.numpy as jnp
from jax import lax
from jax.experimental import pallas as pl
from jax.experimental.pallas import tpu as pltpu
from jax.sharding import PartitionSpec as P

MESH = pl.DeviceIdType.MESH
BF, F32 = jnp.bfloat16, jnp.float32

XL, NY, NZ, NS = 2, 4, 8, 4
HD = 128
G = 3
GC = G * HD
V = 128
VID, TXT = 512, 256
TOK = VID + TXT
D = 3072
WCOL = 12
WB = 48
QC = 768
PIECES = 8
SEMS = 192
SCALE = HD**-0.5
LOG2E = 1.4426950408889634


def dot(a, b, ca=1, cb=0):
    return lax.dot_general(a, b, (((ca,), (cb,)), ((), ())), preferred_element_type=F32)


def kernel(
    vq, vk, vv, tq, tk, tv, qg, kg, gate, wt, go, tgo,
    o_video, o_text, o_w, o_gain,
    qb, kb, vb, dyr, dyb, wbuf, wslot, w48, dout, grads,
    p_s, qn_s, kn_s, knt_s, vt_s, ot_s, dk_a, dv_a, gains,
    tbuf, r1, rbuf, zs, zr, xsum, xr, g_x, g_y, g_z,
    ssem, rsem, lsem,
):
    dp, s = lax.axis_index("dp"), lax.axis_index("seq")
    xl, y, z = dp // (NY * NZ), (dp // NZ) % NY, dp % NZ
    core = s + 1 - 2 * (s % 2)
    part = (s + 2) % NS
    diag = (core + 2) % NS
    seq_peer = {0: s, 1: core, 2: part, 3: diag}

    def ydev(k):
        return (xl * (NY * NZ) + ((y + NY + k) % NY) * NZ + z, s)

    def zdev(k):
        return (xl * (NY * NZ) + y * NZ + (z + NZ + k) % NZ, s)

    dpx = (dp + NY * NZ) % (XL * NY * NZ)
    xdev = (dpx, s)

    def sdev(d):
        return (dp, seq_peer[d])

    def xsdev(d):
        return (dpx, seq_peer[d])

    names = {}
    pending = []
    local = []

    def remote(key, src, dst, dev):
        i = names.setdefault(key, len(names))
        assert i < SEMS
        return pltpu.make_async_remote_copy(
            src_ref=src, dst_ref=dst, send_sem=ssem.at[i], recv_sem=rsem.at[i],
            device_id=dev, device_id_type=MESH,
        )

    def send(key, src, dst, dev):
        copy = remote(key, src, dst, dev)
        copy.start()
        pending.append(copy)

    def arrived(key, dst, dev):
        remote(key, dst, dst, dev).wait_recv()

    def here(src, dst):
        copy = pltpu.make_async_copy(src, dst, lsem.at[len(local)])
        copy.start()
        local.append(copy)
        return copy

    def rows_of(j):
        return pl.ds(pl.multiple_of(j * V, V), V)

    def cols_of(j):
        return pl.ds(pl.multiple_of(j * GC, GC), GC)

    def head_cols(j, h):
        return pl.ds(pl.multiple_of(j * GC + h * HD, HD), HD)

    peers = [sdev(d) for d in (1, 2, 3)] + [xsdev(d) for d in range(NS)]
    peers += [ydev(k) for k in range(1, NY)] + [zdev(k) for k in range(1, NZ)]
    barrier = pltpu.get_barrier_semaphore()
    for dev in peers:
        pl.semaphore_signal(barrier, inc=1, device_id=dev, device_id_type=MESH)

    own_w = here(wt.at[:, cols_of(s)], wslot.at[xl, s])
    own_dy = here(go, dyr.at[rows_of(s)])
    text_dy = here(tgo, dyr.at[pl.ds(VID, TXT)])
    own = []
    for src, tsrc, dst in ((vq, tq, qb), (vk, tk, kb), (vv, tv, vb)):
        own.append(here(src.at[:, cols_of(s)], dst.at[rows_of(s)]))
        own.append(here(tsrc.at[:, cols_of(s)], dst.at[pl.ds(VID, TXT)]))
    pl.semaphore_wait(barrier, len(peers))

    for d in range(NS):
        cols = wt.at[:, cols_of(seq_peer[d])]
        if d:
            send(("w", 0, d), cols, wslot.at[xl, s], sdev(d))
        send(("w", 1, d), cols, wslot.at[xl, s], xsdev(d))

    piece = V // PIECES

    def dy_piece(j, t):
        return dyr.at[pl.ds(pl.multiple_of(j * V + t * piece, piece), piece)]

    def send_in(h):
        for d in (2, 3, 1):
            for n, (src, dst) in enumerate(((vq, qb), (vk, kb), (vv, vb))):
                send(("in", h, d, n), src.at[:, head_cols(seq_peer[d], h)],
                     dst.at[rows_of(s), pl.ds(h * HD, HD)], sdev(d))

    def wait_in(h):
        for d in (2, 3, 1):
            for n, dst in enumerate((qb, kb, vb)):
                arrived(("in", h, d, n), dst.at[rows_of(seq_peer[d]), pl.ds(h * HD, HD)], sdev(d))

    own_w.wait()
    for d in range(NS):
        if d:
            arrived(("w", 0, d), wslot.at[xl, seq_peer[d]], sdev(d))
        arrived(("w", 1, d), wslot.at[1 - xl, seq_peer[d]], xsdev(d))
    for t in range(PIECES):
        send(("dyx", t), go.at[pl.ds(t * piece, piece)], dy_piece(s, t), sdev(2))
    send("dyc", go, dyr.at[rows_of(s)], sdev(1))
    send_in(0)
    for i in range(XL):
        for j in range(NS):
            w48[i, pl.ds(j * WCOL, WCOL), :] = wslot[i, j].astype(F32)[:WCOL]
        wbuf[i, y, z] = w48[i].astype(BF)

    ca, cb = pl.ds(HD, GC - HD), pl.ds(0, HD)

    def blk_a(ky, kz):
        return wbuf.at[:, (y + NY + ky) % NY, (z + NZ + kz) % NZ, :, ca]

    def blk_b(kz):
        return wbuf.at[:, :, (z + NZ + kz) % NZ, :, cb]

    def along_y(kz):
        for k in range(1, NY):
            send(("wya", kz % NZ, k), blk_a(0, kz), blk_a(0, kz), ydev(k))

    for k in range(1, NY):
        mine = wbuf.at[:, y, z, :, cb]
        send(("wyb", k), mine, mine, ydev(k))
    send(("wza+", 0), blk_a(0, 0), blk_a(0, 0), zdev(1))
    send(("wza-", 0), blk_a(0, 0), blk_a(0, 0), zdev(-1))
    along_y(0)
    for k in range(1, NY):
        arrived(("wyb", k), wbuf.at[:, (y + NY - k) % NY, z, :, cb], ydev(-k))
    send(("wzb+", 0), blk_b(0), blk_b(0), zdev(1))
    send(("wzb-", 0), blk_b(0), blk_b(0), zdev(-1))

    def pass_on_dy(t):
        arrived(("dyx", t), dy_piece(part, t), sdev(2))
        send(("dyr", t), dy_piece(part, t), dy_piece(part, t), sdev(1))

    gate_f = gate[...].astype(F32)

    def gated(j, count):
        def body(i, carry):
            at = pl.ds(pl.multiple_of(j * V + i * 32, 32), 32)
            dyb[at, :] = (dyr[at, :].astype(F32) * gate_f).astype(BF)
            return carry
        lax.fori_loop(0, count // 32, body, 0)

    last_p, last_m = NZ // 2, NZ // 2 - 1
    for t in range(last_p):
        arrived(("wza+", t), blk_a(0, -1 - t), zdev(-1))
        if t + 1 < last_p:
            send(("wza+", t + 1), blk_a(0, -1 - t), blk_a(0, -1 - t), zdev(1))
        along_y(-1 - t)
        if t < last_m:
            arrived(("wza-", t), blk_a(0, 1 + t), zdev(1))
            if t + 1 < last_m:
                send(("wza-", t + 1), blk_a(0, 1 + t), blk_a(0, 1 + t), zdev(-1))
            along_y(1 + t)
        arrived(("wzb+", t), blk_b(-1 - t), zdev(-1))
        if t + 1 < last_p:
            send(("wzb+", t + 1), blk_b(-1 - t), blk_b(-1 - t), zdev(1))
        if t < last_m:
            arrived(("wzb-", t), blk_b(1 + t), zdev(1))
            if t + 1 < last_m:
                send(("wzb-", t + 1), blk_b(1 + t), blk_b(1 + t), zdev(-1))
        if t == 0:
            own_dy.wait()
            gated(s, V)
        if t == 1:
            text_dy.wait()
            gated(NS, TXT)
        if t == 2:
            arrived("dyc", dyr.at[rows_of(core)], sdev(1))
            gated(core, V)
            send_in(1)
    send_in(2)
    for t in range(PIECES):
        pass_on_dy(t)
    gated(part, V)

    for copy in own:
        copy.wait()
    q_gain, k_gain = qg[...], kg[...]
    gains[...] = jnp.zeros_like(gains)

    def norm(x):
        return lax.rsqrt(jnp.sum(x * x, axis=-1, keepdims=True) * (1.0 / HD) + 1e-06)

    def through_norm(x, r, u):
        return r * u - x * (r * r * r) * (jnp.sum(u * x, axis=-1, keepdims=True) * (1.0 / HD))

    def fwd(h):
        cols = pl.ds(h * HD, HD)
        qf = qb[:, cols].astype(F32)
        qn_s[h] = (qf * norm(qf) * q_gain).astype(BF)
        kf = kb[:, cols].astype(F32)
        kn = kf * norm(kf) * k_gain
        kn_s[h] = kn.astype(BF)
        knt_s[h] = kn.T.astype(BF)
        vt_s[...] = vb[:, cols].astype(F32).T.astype(BF)

        def chunk(c, carry):
            at = pl.ds(pl.multiple_of(c * QC, QC), QC)
            e = jnp.exp2(dot(kn_s[h], qn_s[h, at, :], 1, 1) * (SCALE * LOG2E))
            p = e * (1.0 / jnp.sum(e, axis=0, keepdims=True))
            p_s[h, :, at] = p
            ot_s[:, at] = dot(vt_s[...], p.astype(BF)).astype(BF)
            return carry
        lax.fori_loop(0, TOK // QC, chunk, 0)

    def bwd(h):
        cols = pl.ds(h * HD, HD)
        dk_a[...] = jnp.zeros_like(dk_a)
        dv_a[...] = jnp.zeros_like(dv_a)

        def chunk(c, carry):
            at = pl.ds(pl.multiple_of(c * QC, QC), QC)
            do = dout[at, cols]
            p = p_s[h, :, at]
            dv_a[...] += dot(p.astype(BF), do)
            dpr = dot(vb[:, cols], do, 1, 1)
            delta = jnp.sum(p * dpr, axis=0, keepdims=True)
            ds = (p * (dpr - delta)).astype(BF)
            dk_a[...] += dot(ds, qn_s[h, at, :])
            dqn = dot(knt_s[h], ds).T * SCALE
            x = qb[at, cols].astype(F32)
            r = norm(x)
            grads[h, 0, at, :] = through_norm(x, r, dqn * q_gain).astype(BF)
            gains[0:1, :] += jnp.sum(dqn * x * r, axis=0, keepdims=True)
            return carry
        lax.fori_loop(0, TOK // QC, chunk, 0)
        dkn = dk_a[...] * SCALE
        x = kb[:, cols].astype(F32)
        r = norm(x)
        grads[h, 1] = through_norm(x, r, dkn * k_gain).astype(BF)
        gains[1:2, :] += jnp.sum(dkn * x * r, axis=0, keepdims=True)
        grads[h, 2] = dv_a[...].astype(BF)

    lo, hi = pl.ds(0, HD // 2), pl.ds(HD // 2, HD // 2)

    def term(h):
        def body(i, carry):
            at = pl.ds(pl.multiple_of(i * NY * GC, NY * GC), NY * GC)
            t = dot(ot_s[...], dyb[:, at]).astype(BF)
            for j in range(NY):
                tbuf[h, i, j] = t[:, j * GC:(j + 1) * GC]
            return carry
        lax.fori_loop(0, XL, body, 0)
        far = tbuf.at[h, :, (y + 2) % NY]
        send(("ty+", h), far.at[:, lo], r1.at[h, 0], ydev(1))
        send(("ty-", h), far.at[:, hi], r1.at[h, 1], ydev(-1))

    def y_mid(h):
        for i, half, k, key in ((0, lo, 1, "+"), (1, hi, -1, "-")):
            arrived(("ty" + key, h), r1.at[h, i], ydev(-k))
            to = (y + NY + k) % NY
            for j in range(XL):
                both = tbuf[h, j, to, half].astype(F32) + r1[h, i, j].astype(F32)
                tbuf[h, j, to, half] = both.astype(BF)
            send(("tyy" + key, h), tbuf.at[h, :, to], rbuf.at[h, i], ydev(k))

    text = pl.ds(VID, TXT)
    out_local = []

    def send_out(h):
        to = head_cols(s, h)
        send(("text", h, 2), grads.at[h, :, text], o_text.at[:, :, to], sdev(2))
        for d in (2, 3):
            send(("out", h, d), grads.at[h, :, rows_of(seq_peer[d])], o_video.at[:, :, to], sdev(d))
        send(("text", h, 1), grads.at[h, :, text], o_text.at[:, :, to], sdev(1))
        send(("out", h, 1), grads.at[h, :, rows_of(seq_peer[1])], o_video.at[:, :, to], sdev(1))
        out_local.append(here(grads.at[h, :, rows_of(s)], o_video.at[:, :, to]))
        out_local.append(here(grads.at[h, :, text], o_text.at[:, :, to]))

    def y_sum(h):
        arrived(("tyy+", h), rbuf.at[h, 0], ydev(-1))
        arrived(("tyy-", h), rbuf.at[h, 1], ydev(1))
        for i in range(XL):
            total = tbuf[h, i, y].astype(F32) + rbuf[h, 0, i].astype(F32) + rbuf[h, 1, i].astype(F32)
            zs[h, :, i] = total.T.reshape(NZ, WB, HD).astype(BF)
        for k in range(1, NZ):
            send(("tz", h, k), zs.at[h, (z + k) % NZ], zr.at[h, k - 1], zdev(k))

    wait_in(0)
    fwd(0)
    for t in range(PIECES):
        arrived(("dyr", t), dy_piece(diag, t), sdev(1))
    gated(diag, V)
    term(0)
    for kz in range(NZ):
        for k in range(1, NY):
            arrived(("wya", kz, k), blk_a(-k, kz), ydev(-k))

    dout[...] = dot(dyb[...], wbuf[...].reshape(D, GC)).astype(BF)

    y_mid(0)
    bwd(0)
    send_out(0)
    wait_in(1)
    fwd(1)
    term(1)
    wait_in(2)
    fwd(2)
    term(2)
    bwd(1)
    send_out(1)
    y_mid(1)
    y_sum(0)
    bwd(2)
    send_out(2)

    g_y[y] = gains[...]
    for k in range(1, NY):
        send(("gy", k), g_y.at[y], g_y.at[y], ydev(k))

    def pass_on_text(h):
        at = o_text.at[:, :, head_cols(part, h)]
        arrived(("text", h, 2), at, sdev(2))
        send(("textr", h), at, at, sdev(1))

    def z_sum(h):
        for k in range(1, NZ):
            arrived(("tz", h, k), zr.at[h, k - 1], zdev(-k))
        total = zs[h, z].astype(F32)
        for k in range(1, NZ):
            total += zr[h, k - 1].astype(F32)
        xsum[:, :, h * HD:(h + 1) * HD] = total

    y_mid(2)
    y_sum(1)
    y_sum(2)
    for k in range(1, NY):
        arrived(("gy", k), g_y.at[(y + NY - k) % NY], ydev(-k))
    g_z[z] = (g_y[0] + g_y[1]) + (g_y[2] + g_y[3])
    for k in range(1, NZ):
        send(("gz", k), g_z.at[z], g_z.at[z], zdev(k))
    z_sum(0)
    z_sum(1)
    for k in range(1, NZ):
        arrived(("gz", k), g_z.at[(z + NZ - k) % NZ], zdev(-k))
    total = g_z[0]
    for k in range(1, NZ):
        total += g_z[k]
    g_x[xl, s] = total
    for d in range(NS):
        if d:
            send(("gx", 0, d), g_x.at[xl, s], g_x.at[xl, s], sdev(d))
        send(("gx", 1, d), g_x.at[xl, s], g_x.at[xl, s], xsdev(d))
    z_sum(2)
    send("tx", xsum.at[1 - xl], xr, xdev)
    for h in range(G):
        pass_on_text(h)
    for d in range(NS):
        if d:
            arrived(("gx", 0, d), g_x.at[xl, seq_peer[d]], sdev(d))
        arrived(("gx", 1, d), g_x.at[1 - xl, seq_peer[d]], xsdev(d))
    total = g_x[0, 0]
    for j in range(1, XL * NS):
        total += g_x[j // NS, j % NS]
    o_gain[...] = total
    arrived("tx", xr, xdev)
    o_w[...] = xsum[xl] + xr[...]

    for h in range(G):
        arrived(("text", h, 1), o_text.at[:, :, head_cols(core, h)], sdev(1))
        arrived(("textr", h), o_text.at[:, :, head_cols(diag, h)], sdev(1))
        for d in (1, 2, 3):
            arrived(("out", h, d), o_video.at[:, :, head_cols(seq_peer[d], h)], sdev(d))
    for copy in out_local:
        copy.wait()
    for copy in pending:
        copy.wait_send()


def shards(video_q, video_k, video_v, text_q, text_k, text_v, q_gain, k_gain, gate, out_weight, grad_out, text_grad_out):
    wt = jnp.pad(out_weight.T, ((0, 16 - WCOL), (0, 0)))
    hbm = pl.BlockSpec(memory_space=pl.ANY)
    vmem = pl.BlockSpec(memory_space=pltpu.VMEM)
    video, text, w, gains = pl.pallas_call(
        kernel,
        out_shape=[
            jax.ShapeDtypeStruct((3, V, NS * GC), BF),
            jax.ShapeDtypeStruct((3, TXT, NS * GC), BF),
            jax.ShapeDtypeStruct((WB, GC), F32),
            jax.ShapeDtypeStruct((8, HD), F32),
        ],
        in_specs=[hbm] * 6 + [vmem] * 3 + [hbm] * 3,
        out_specs=[hbm, hbm, vmem, vmem],
        scratch_shapes=[
            pltpu.VMEM((TOK, GC), BF),
            pltpu.VMEM((TOK, GC), BF),
            pltpu.VMEM((TOK, GC), BF),
            pltpu.VMEM((TOK, D), BF),
            pltpu.VMEM((TOK, D), BF),
            pltpu.VMEM((XL, NY, NZ, WB, GC), BF),
            pltpu.VMEM((XL, NS, 16, GC), BF),
            pltpu.VMEM((XL, WB, GC), F32),
            pltpu.VMEM((TOK, GC), BF),
            pltpu.VMEM((G, 3, TOK, HD), BF),
            pltpu.VMEM((G, TOK, TOK), F32),
            pltpu.VMEM((G, TOK, HD), BF),
            pltpu.VMEM((G, TOK, HD), BF),
            pltpu.VMEM((G, HD, TOK), BF),
            pltpu.VMEM((HD, TOK), BF),
            pltpu.VMEM((HD, TOK), BF),
            pltpu.VMEM((TOK, HD), F32),
            pltpu.VMEM((TOK, HD), F32),
            pltpu.VMEM((8, HD), F32),
            pltpu.VMEM((G, XL, NY, HD, GC), BF),
            pltpu.VMEM((G, 2, XL, HD // 2, GC), BF),
            pltpu.VMEM((G, 2, XL, HD, GC), BF),
            pltpu.VMEM((G, NZ, XL, WB, HD), BF),
            pltpu.VMEM((G, NZ - 1, XL, WB, HD), BF),
            pltpu.VMEM((XL, WB, GC), F32),
            pltpu.VMEM((WB, GC), F32),
            pltpu.VMEM((XL, NS, 8, HD), F32),
            pltpu.VMEM((NY, 8, HD), F32),
            pltpu.VMEM((NZ, 8, HD), F32),
            pltpu.SemaphoreType.DMA((SEMS,)),
            pltpu.SemaphoreType.DMA((SEMS,)),
            pltpu.SemaphoreType.DMA((16,)),
        ],
        compiler_params=pltpu.CompilerParams(
            collective_id=0, has_side_effects=True, vmem_limit_bytes=62 << 20
        ),
        cost_estimate=pl.CostEstimate(flops=7 * 10**9, bytes_accessed=14 << 20, transcendentals=1 << 21),
    )(
        video_q, video_k, video_v, text_q, text_k, text_v,
        q_gain.reshape(1, HD), k_gain.reshape(1, HD), gate, wt, grad_out, text_grad_out,
    )
    return (
        video[0], video[1], video[2], text[0], text[1], text[2],
        w.T, gains[0], gains[1],
    )


def solution(mesh):
    rows, clip = P(("dp", "seq"), None), P("dp", None)
    return jax.shard_map(
        shards,
        mesh=mesh,
        in_specs=(rows,) * 3 + (clip,) * 3 + (P(), P(), clip, P(None, ("dp", "seq")), rows, clip),
        out_specs=(rows,) * 3 + (clip,) * 3 + (P("seq", "dp"), P(), P()),
        check_vma=False,
    )
```

```python
import functools

import jax
import jax.numpy as jnp
from jax import lax
from jax.experimental import pallas as pl
from jax.experimental.pallas import tpu as pltpu
from jax.sharding import PartitionSpec as P

MESH = pl.DeviceIdType.MESH
BF, F32 = jnp.bfloat16, jnp.float32

XL, NY, NZ, NS = 2, 4, 8, 4
HD = 128
G = 3
GC = G * HD
V = 128
VID, TXT = 512, 256
TOK = VID + TXT
D = 3072
WCOL = 12
WB = 48
QC = 768
PIECES = 8
SEMS = 192
EARLY = 4
SCALE = HD**-0.5
LOG2E = 1.4426950408889634


def dot(a, b, ca=1, cb=0):
    return lax.dot_general(a, b, (((ca,), (cb,)), ((), ())), preferred_element_type=F32)


def kernel(
    vq, vk, vv, tq, tk, tv, qg, kg, gate, w_own, go, tgo,
    o_video, o_text, o_w, o_gain,
    wt, qb, kb, vb, dyr, dyb, wbuf, wslot, w48, dout, grads,
    p_s, qn_s, kn_s, knt_s, vt_s, ot_s, dk_a, dv_a, gains,
    tbuf, r1, rbuf, zs, zr, xsum, xr, g_x, g_y, g_z,
    ssem, rsem, lsem,
):
    dp, s = lax.axis_index("dp"), lax.axis_index("seq")
    xl, y, z = dp // (NY * NZ), (dp // NZ) % NY, dp % NZ
    core = s + 1 - 2 * (s % 2)
    part = (s + 2) % NS
    diag = (core + 2) % NS
    seq_peer = {0: s, 1: core, 2: part, 3: diag}

    def ydev(k):
        return (xl * (NY * NZ) + ((y + NY + k) % NY) * NZ + z, s)

    def zdev(k):
        return (xl * (NY * NZ) + y * NZ + (z + NZ + k) % NZ, s)

    dpx = (dp + NY * NZ) % (XL * NY * NZ)
    xdev = (dpx, s)

    def sdev(d):
        return (dp, seq_peer[d])

    def xsdev(d):
        return (dpx, seq_peer[d])

    names = {}
    pending = []
    local = []

    def remote(key, src, dst, dev):
        i = names.setdefault(key, len(names))
        assert i < SEMS
        return pltpu.make_async_remote_copy(
            src_ref=src, dst_ref=dst, send_sem=ssem.at[i], recv_sem=rsem.at[i],
            device_id=dev, device_id_type=MESH,
        )

    def send(key, src, dst, dev):
        copy = remote(key, src, dst, dev)
        copy.start()
        pending.append(copy)

    def arrived(key, dst, dev):
        remote(key, dst, dst, dev).wait_recv()

    def here(src, dst):
        copy = pltpu.make_async_copy(src, dst, lsem.at[len(local)])
        copy.start()
        local.append(copy)
        return copy

    def rows_of(j):
        return pl.ds(pl.multiple_of(j * V, V), V)

    def cols_of(j):
        return pl.ds(pl.multiple_of(j * GC, GC), GC)

    def head_cols(j, h):
        return pl.ds(pl.multiple_of(j * GC + h * HD, HD), HD)

    peers = [sdev(d) for d in (1, 2, 3)] + [xsdev(d) for d in range(NS)]
    peers += [ydev(k) for k in range(1, NY)] + [zdev(k) for k in range(1, NZ)]
    barrier = pltpu.get_barrier_semaphore()
    for dev in peers:
        pl.semaphore_signal(barrier, inc=1, device_id=dev, device_id_type=MESH)

    wt[...] = jnp.zeros_like(wt)
    wt[pl.ds(0, WCOL), :] = w_own[...]
    own_w = here(wt.at[:, cols_of(s)], wslot.at[xl, s])
    own_dy = here(go, dyr.at[rows_of(s)])
    text_dy = here(tgo, dyr.at[pl.ds(VID, TXT)])
    own = []
    for src, tsrc, dst in ((vq, tq, qb), (vk, tk, kb), (vv, tv, vb)):
        own.append(here(src.at[:, cols_of(s)], dst.at[rows_of(s)]))
        own.append(here(tsrc.at[:, cols_of(s)], dst.at[pl.ds(VID, TXT)]))
    pl.semaphore_wait(barrier, len(peers))

    for d in range(NS):
        cols = wt.at[:, cols_of(seq_peer[d])]
        if d:
            send(("w", 0, d), cols, wslot.at[xl, s], sdev(d))
        send(("w", 1, d), cols, wslot.at[xl, s], xsdev(d))

    piece = V // PIECES

    def dy_piece(j, t):
        return dyr.at[pl.ds(pl.multiple_of(j * V + t * piece, piece), piece)]

    for t in range(EARLY):
        send(("dyx", t), go.at[pl.ds(t * piece, piece)], dy_piece(s, t), sdev(2))

    def send_in(h):
        for d in (2, 3, 1):
            for n, (src, dst) in enumerate(((vq, qb), (vk, kb), (vv, vb))):
                send(("in", h, d, n), src.at[:, head_cols(seq_peer[d], h)],
                     dst.at[rows_of(s), pl.ds(h * HD, HD)], sdev(d))

    def wait_in(h):
        for d in (2, 3, 1):
            for n, dst in enumerate((qb, kb, vb)):
                arrived(("in", h, d, n), dst.at[rows_of(seq_peer[d]), pl.ds(h * HD, HD)], sdev(d))

    own_w.wait()
    for d in range(NS):
        if d:
            arrived(("w", 0, d), wslot.at[xl, seq_peer[d]], sdev(d))
        arrived(("w", 1, d), wslot.at[1 - xl, seq_peer[d]], xsdev(d))
    for t in range(EARLY, PIECES):
        send(("dyx", t), go.at[pl.ds(t * piece, piece)], dy_piece(s, t), sdev(2))
    send("dyc", go, dyr.at[rows_of(s)], sdev(1))
    send_in(0)
    for i in range(XL):
        for j in range(NS):
            w48[i, pl.ds(j * WCOL, WCOL), :] = wslot[i, j].astype(F32)[:WCOL]
        wbuf[i, y, z] = w48[i].astype(BF)

    ca, cb = pl.ds(HD, GC - HD), pl.ds(0, HD)

    def blk_a(ky, kz):
        return wbuf.at[:, (y + NY + ky) % NY, (z + NZ + kz) % NZ, :, ca]

    def blk_b(kz):
        return wbuf.at[:, :, (z + NZ + kz) % NZ, :, cb]

    def along_y(kz):
        for k in range(1, NY):
            send(("wya", kz % NZ, k), blk_a(0, kz), blk_a(0, kz), ydev(k))

    for k in range(1, NY):
        mine = wbuf.at[:, y, z, :, cb]
        send(("wyb", k), mine, mine, ydev(k))
    send(("wza+", 0), blk_a(0, 0), blk_a(0, 0), zdev(1))
    send(("wza-", 0), blk_a(0, 0), blk_a(0, 0), zdev(-1))
    along_y(0)
    for k in range(1, NY):
        arrived(("wyb", k), wbuf.at[:, (y + NY - k) % NY, z, :, cb], ydev(-k))
    send(("wzb+", 0), blk_b(0), blk_b(0), zdev(1))
    send(("wzb-", 0), blk_b(0), blk_b(0), zdev(-1))

    def pass_on_dy(t):
        arrived(("dyx", t), dy_piece(part, t), sdev(2))
        send(("dyr", t), dy_piece(part, t), dy_piece(part, t), sdev(1))

    gate_f = gate[...].astype(F32)

    def gated(j, count):
        def body(i, carry):
            at = pl.ds(pl.multiple_of(j * V + i * 32, 32), 32)
            dyb[at, :] = (dyr[at, :].astype(F32) * gate_f).astype(BF)
            return carry
        lax.fori_loop(0, count // 32, body, 0)

    last_p, last_m = NZ // 2, NZ // 2 - 1
    for t in range(last_p):
        arrived(("wza+", t), blk_a(0, -1 - t), zdev(-1))
        if t + 1 < last_p:
            send(("wza+", t + 1), blk_a(0, -1 - t), blk_a(0, -1 - t), zdev(1))
        along_y(-1 - t)
        if t < last_m:
            arrived(("wza-", t), blk_a(0, 1 + t), zdev(1))
            if t + 1 < last_m:
                send(("wza-", t + 1), blk_a(0, 1 + t), blk_a(0, 1 + t), zdev(-1))
            along_y(1 + t)
        arrived(("wzb+", t), blk_b(-1 - t), zdev(-1))
        if t + 1 < last_p:
            send(("wzb+", t + 1), blk_b(-1 - t), blk_b(-1 - t), zdev(1))
        if t < last_m:
            arrived(("wzb-", t), blk_b(1 + t), zdev(1))
            if t + 1 < last_m:
                send(("wzb-", t + 1), blk_b(1 + t), blk_b(1 + t), zdev(-1))
        if t == 0:
            own_dy.wait()
            gated(s, V)
        if t == 1:
            text_dy.wait()
            gated(NS, TXT)
        if t == 2:
            arrived("dyc", dyr.at[rows_of(core)], sdev(1))
            gated(core, V)
            send_in(1)
    send_in(2)
    for t in range(PIECES):
        pass_on_dy(t)
    gated(part, V)

    for copy in own:
        copy.wait()
    q_gain, k_gain = qg[...], kg[...]
    gains[...] = jnp.zeros_like(gains)

    def norm(x):
        return lax.rsqrt(jnp.sum(x * x, axis=-1, keepdims=True) * (1.0 / HD) + 1e-06)

    def through_norm(x, r, u):
        return r * u - x * (r * r * r) * (jnp.sum(u * x, axis=-1, keepdims=True) * (1.0 / HD))

    def fwd(h):
        cols = pl.ds(h * HD, HD)
        qf = qb[:, cols].astype(F32)
        qn_s[h] = (qf * norm(qf) * q_gain).astype(BF)
        kf = kb[:, cols].astype(F32)
        kn = kf * norm(kf) * k_gain
        kn_s[h] = kn.astype(BF)
        knt_s[h] = kn.T.astype(BF)
        vt_s[...] = vb[:, cols].astype(F32).T.astype(BF)

        def chunk(c, carry):
            at = pl.ds(pl.multiple_of(c * QC, QC), QC)
            e = jnp.exp2(dot(kn_s[h], qn_s[h, at, :], 1, 1) * (SCALE * LOG2E))
            p = e * (1.0 / jnp.sum(e, axis=0, keepdims=True))
            p_s[h, :, at] = p
            ot_s[:, at] = dot(vt_s[...], p.astype(BF)).astype(BF)
            return carry
        lax.fori_loop(0, TOK // QC, chunk, 0)

    def bwd(h):
        cols = pl.ds(h * HD, HD)
        dk_a[...] = jnp.zeros_like(dk_a)
        dv_a[...] = jnp.zeros_like(dv_a)

        def chunk(c, carry):
            at = pl.ds(pl.multiple_of(c * QC, QC), QC)
            do = dout[at, cols]
            p = p_s[h, :, at]
            dv_a[...] += dot(p.astype(BF), do)
            dpr = dot(vb[:, cols], do, 1, 1)
            delta = jnp.sum(p * dpr, axis=0, keepdims=True)
            ds = (p * (dpr - delta)).astype(BF)
            dk_a[...] += dot(ds, qn_s[h, at, :])
            dqn = dot(knt_s[h], ds).T * SCALE
            x = qb[at, cols].astype(F32)
            r = norm(x)
            grads[h, 0, at, :] = through_norm(x, r, dqn * q_gain).astype(BF)
            gains[0:1, :] += jnp.sum(dqn * x * r, axis=0, keepdims=True)
            return carry
        lax.fori_loop(0, TOK // QC, chunk, 0)
        dkn = dk_a[...] * SCALE
        x = kb[:, cols].astype(F32)
        r = norm(x)
        grads[h, 1] = through_norm(x, r, dkn * k_gain).astype(BF)
        gains[1:2, :] += jnp.sum(dkn * x * r, axis=0, keepdims=True)
        grads[h, 2] = dv_a[...].astype(BF)

    lo, hi = pl.ds(0, HD // 2), pl.ds(HD // 2, HD // 2)

    def term(h):
        def body(i, carry):
            at = pl.ds(pl.multiple_of(i * NY * GC, NY * GC), NY * GC)
            t = dot(ot_s[...], dyb[:, at]).astype(BF)
            for j in range(NY):
                tbuf[h, i, j] = t[:, j * GC:(j + 1) * GC]
            return carry
        lax.fori_loop(0, XL, body, 0)
        far = tbuf.at[h, :, (y + 2) % NY]
        send(("ty+", h), far.at[:, lo], r1.at[h, 0], ydev(1))
        send(("ty-", h), far.at[:, hi], r1.at[h, 1], ydev(-1))

    def y_mid(h):
        for i, half, k, key in ((0, lo, 1, "+"), (1, hi, -1, "-")):
            arrived(("ty" + key, h), r1.at[h, i], ydev(-k))
            to = (y + NY + k) % NY
            for j in range(XL):
                both = tbuf[h, j, to, half].astype(F32) + r1[h, i, j].astype(F32)
                tbuf[h, j, to, half] = both.astype(BF)
            send(("tyy" + key, h), tbuf.at[h, :, to], rbuf.at[h, i], ydev(k))

    text = pl.ds(VID, TXT)
    out_local = []

    def send_out(h):
        to = head_cols(s, h)
        send(("text", h, 2), grads.at[h, :, text], o_text.at[:, :, to], sdev(2))
        for d in (2, 3):
            send(("out", h, d), grads.at[h, :, rows_of(seq_peer[d])], o_video.at[:, :, to], sdev(d))
        send(("text", h, 1), grads.at[h, :, text], o_text.at[:, :, to], sdev(1))
        send(("out", h, 1), grads.at[h, :, rows_of(seq_peer[1])], o_video.at[:, :, to], sdev(1))
        out_local.append(here(grads.at[h, :, rows_of(s)], o_video.at[:, :, to]))
        out_local.append(here(grads.at[h, :, text], o_text.at[:, :, to]))

    def y_sum(h):
        arrived(("tyy+", h), rbuf.at[h, 0], ydev(-1))
        arrived(("tyy-", h), rbuf.at[h, 1], ydev(1))
        for i in range(XL):
            total = tbuf[h, i, y].astype(F32) + rbuf[h, 0, i].astype(F32) + rbuf[h, 1, i].astype(F32)
            zs[h, :, i] = total.T.reshape(NZ, WB, HD).astype(BF)
        for k in range(1, NZ):
            send(("tz", h, k), zs.at[h, (z + k) % NZ], zr.at[h, k - 1], zdev(k))

    wait_in(0)
    fwd(0)
    for t in range(PIECES):
        arrived(("dyr", t), dy_piece(diag, t), sdev(1))
    gated(diag, V)
    term(0)
    for kz in range(NZ):
        for k in range(1, NY):
            arrived(("wya", kz, k), blk_a(-k, kz), ydev(-k))

    dout[...] = dot(dyb[...], wbuf[...].reshape(D, GC)).astype(BF)

    bwd(0)
    send_out(0)
    y_mid(0)
    wait_in(1)
    fwd(1)
    term(1)
    wait_in(2)
    fwd(2)
    term(2)
    bwd(1)
    send_out(1)
    y_mid(1)
    y_sum(0)
    bwd(2)
    send_out(2)

    g_y[y] = gains[...]
    for k in range(1, NY):
        send(("gy", k), g_y.at[y], g_y.at[y], ydev(k))

    def pass_on_text(h):
        at = o_text.at[:, :, head_cols(part, h)]
        arrived(("text", h, 2), at, sdev(2))
        send(("textr", h), at, at, sdev(1))

    def z_sum(h):
        for k in range(1, NZ):
            arrived(("tz", h, k), zr.at[h, k - 1], zdev(-k))
        total = zs[h, z].astype(F32)
        for k in range(1, NZ):
            total += zr[h, k - 1].astype(F32)
        xsum[:, :, h * HD:(h + 1) * HD] = total

    y_mid(2)
    pass_on_text(0)
    y_sum(1)
    y_sum(2)
    for k in range(1, NY):
        arrived(("gy", k), g_y.at[(y + NY - k) % NY], ydev(-k))
    g_z[z] = (g_y[0] + g_y[1]) + (g_y[2] + g_y[3])
    for k in range(1, NZ):
        send(("gz", k), g_z.at[z], g_z.at[z], zdev(k))
    pass_on_text(1)
    z_sum(0)
    z_sum(1)
    for k in range(1, NZ):
        arrived(("gz", k), g_z.at[(z + NZ - k) % NZ], zdev(-k))
    total = g_z[0]
    for k in range(1, NZ):
        total += g_z[k]
    g_x[xl, s] = total
    for d in range(NS):
        if d:
            send(("gx", 0, d), g_x.at[xl, s], g_x.at[xl, s], sdev(d))
        send(("gx", 1, d), g_x.at[xl, s], g_x.at[xl, s], xsdev(d))
    z_sum(2)
    send("tx", xsum.at[1 - xl], xr, xdev)
    pass_on_text(2)
    for d in range(NS):
        if d:
            arrived(("gx", 0, d), g_x.at[xl, seq_peer[d]], sdev(d))
        arrived(("gx", 1, d), g_x.at[1 - xl, seq_peer[d]], xsdev(d))
    total = g_x[0, 0]
    for j in range(1, XL * NS):
        total += g_x[j // NS, j % NS]
    o_gain[...] = total
    arrived("tx", xr, xdev)
    o_w[...] = xsum[xl] + xr[...]

    for h in range(G):
        arrived(("text", h, 1), o_text.at[:, :, head_cols(core, h)], sdev(1))
        arrived(("textr", h), o_text.at[:, :, head_cols(diag, h)], sdev(1))
        for d in (1, 2, 3):
            arrived(("out", h, d), o_video.at[:, :, head_cols(seq_peer[d], h)], sdev(d))
    for copy in out_local:
        copy.wait()
    for copy in pending:
        copy.wait_send()


def place(video, text, w, gains, *rest):
    outs, (row_q, row_k, sems) = rest[:9], rest[9:]
    row_q[...] = gains[0:1, :]
    row_k[...] = gains[1:2, :]
    parts = [(text.at[n], outs[3 + n]) for n in range(3)] + [(video.at[n], outs[n]) for n in range(3)]
    parts += [(w, outs[6]), (row_q, outs[7]), (row_k, outs[8])]
    copies = [pltpu.make_async_copy(src, dst, sems.at[n]) for n, (src, dst) in enumerate(parts)]
    for copy in copies:
        copy.start()
    for copy in copies:
        copy.wait()


def shards(video_q, video_k, video_v, text_q, text_k, text_v, q_gain, k_gain, gate, out_weight, grad_out, text_grad_out):
    hbm = pl.BlockSpec(memory_space=pltpu.HBM)
    vmem = pl.BlockSpec(memory_space=pltpu.VMEM)
    video, text, w, gains = pl.pallas_call(
        kernel,
        out_shape=[
            jax.ShapeDtypeStruct((3, V, NS * GC), BF),
            jax.ShapeDtypeStruct((3, TXT, NS * GC), BF),
            jax.ShapeDtypeStruct((WB, GC), F32),
            jax.ShapeDtypeStruct((8, HD), F32),
        ],
        in_specs=[hbm] * 6 + [vmem] * 4 + [hbm] * 2,
        out_specs=[vmem] * 4,
        scratch_shapes=[
            pltpu.VMEM((16, NS * GC), BF),
            pltpu.VMEM((TOK, GC), BF),
            pltpu.VMEM((TOK, GC), BF),
            pltpu.VMEM((TOK, GC), BF),
            pltpu.VMEM((TOK, D), BF),
            pltpu.VMEM((TOK, D), BF),
            pltpu.VMEM((XL, NY, NZ, WB, GC), BF),
            pltpu.VMEM((XL, NS, 16, GC), BF),
            pltpu.VMEM((XL, WB, GC), F32),
            pltpu.VMEM((TOK, GC), BF),
            pltpu.VMEM((G, 3, TOK, HD), BF),
            pltpu.VMEM((G, TOK, TOK), F32),
            pltpu.VMEM((G, TOK, HD), BF),
            pltpu.VMEM((G, TOK, HD), BF),
            pltpu.VMEM((G, HD, TOK), BF),
            pltpu.VMEM((HD, TOK), BF),
            pltpu.VMEM((HD, TOK), BF),
            pltpu.VMEM((TOK, HD), F32),
            pltpu.VMEM((TOK, HD), F32),
            pltpu.VMEM((8, HD), F32),
            pltpu.VMEM((G, XL, NY, HD, GC), BF),
            pltpu.VMEM((G, 2, XL, HD // 2, GC), BF),
            pltpu.VMEM((G, 2, XL, HD, GC), BF),
            pltpu.VMEM((G, NZ, XL, WB, HD), BF),
            pltpu.VMEM((G, NZ - 1, XL, WB, HD), BF),
            pltpu.VMEM((XL, WB, GC), F32),
            pltpu.VMEM((WB, GC), F32),
            pltpu.VMEM((XL, NS, 8, HD), F32),
            pltpu.VMEM((NY, 8, HD), F32),
            pltpu.VMEM((NZ, 8, HD), F32),
            pltpu.SemaphoreType.DMA((SEMS,)),
            pltpu.SemaphoreType.DMA((SEMS,)),
            pltpu.SemaphoreType.DMA((16,)),
        ],
        compiler_params=pltpu.CompilerParams(
            collective_id=0, has_side_effects=True, vmem_limit_bytes=54 << 20
        ),
        cost_estimate=pl.CostEstimate(flops=7 * 10**9, bytes_accessed=14 << 20, transcendentals=1 << 21),
    )(
        video_q, video_k, video_v, text_q, text_k, text_v,
        q_gain.reshape(1, HD), k_gain.reshape(1, HD), gate, out_weight.T, grad_out, text_grad_out,
    )
    rows = [jax.ShapeDtypeStruct((V, NS * GC), BF)] * 3 + [jax.ShapeDtypeStruct((TXT, NS * GC), BF)] * 3
    outs = pl.pallas_call(
        place,
        out_shape=rows + [jax.ShapeDtypeStruct((WB, GC), F32)] + [jax.ShapeDtypeStruct((1, HD), F32)] * 2,
        in_specs=[vmem] * 4,
        out_specs=[hbm] * 9,
        scratch_shapes=[pltpu.VMEM((1, HD), F32), pltpu.VMEM((1, HD), F32), pltpu.SemaphoreType.DMA((9,))],
        cost_estimate=pl.CostEstimate(flops=0, bytes_accessed=7 << 20, transcendentals=0),
    )(video, text, w, gains)
    return (*outs[:6], outs[6].T, outs[7].reshape(HD), outs[8].reshape(HD))


def solution(mesh):
    rows, clip = P(("dp", "seq"), None), P("dp", None)
    return jax.shard_map(
        shards,
        mesh=mesh,
        in_specs=(rows,) * 3 + (clip,) * 3 + (P(), P(), clip, P(None, ("dp", "seq")), rows, clip),
        out_specs=(rows,) * 3 + (clip,) * 3 + (P("seq", "dp"), P(), P()),
        check_vma=False,
    )
```

```python
import functools

import jax
import jax.numpy as jnp
from jax import lax
from jax.experimental import pallas as pl
from jax.experimental.pallas import tpu as pltpu
from jax.sharding import PartitionSpec as P

MESH = pl.DeviceIdType.MESH
BF, F32 = jnp.bfloat16, jnp.float32

XL, NY, NZ, NS = 2, 4, 8, 4
HD = 128
G = 3
GC = G * HD
V = 128
VID, TXT = 512, 256
TOK = VID + TXT
D = 3072
WCOL = 12
WB = 48
QC = 768
PIECES = 8
SEMS = 192
EARLY = 4
SCALE = HD**-0.5
LOG2E = 1.4426950408889634


def dot(a, b, ca=1, cb=0):
    return lax.dot_general(a, b, (((ca,), (cb,)), ((), ())), preferred_element_type=F32)


def kernel(
    vq, vk, vv, tq, tk, tv, qg, kg, gate, w_own, go, tgo,
    o_video, o_text, o_w, o_gain,
    wt, qb, kb, vb, dyr, dyb, wbuf, wslot, w48, dout, grads,
    p_s, qn_s, kn_s, knt_s, vt_s, ot_s, dk_a, dv_a, gains,
    tbuf, r1, rbuf, zs, zr, xsum, xr, g_x, g_y, g_z,
    ssem, rsem, lsem,
):
    dp, s = lax.axis_index("dp"), lax.axis_index("seq")
    xl, y, z = dp // (NY * NZ), (dp // NZ) % NY, dp % NZ
    core = s + 1 - 2 * (s % 2)
    part = (s + 2) % NS
    diag = (core + 2) % NS
    seq_peer = {0: s, 1: core, 2: part, 3: diag}

    def ydev(k):
        return (xl * (NY * NZ) + ((y + NY + k) % NY) * NZ + z, s)

    def zdev(k):
        return (xl * (NY * NZ) + y * NZ + (z + NZ + k) % NZ, s)

    dpx = (dp + NY * NZ) % (XL * NY * NZ)
    xdev = (dpx, s)

    def sdev(d):
        return (dp, seq_peer[d])

    def xsdev(d):
        return (dpx, seq_peer[d])

    names = {}
    pending = []
    local = []

    def remote(key, src, dst, dev):
        i = names.setdefault(key, len(names))
        assert i < SEMS
        return pltpu.make_async_remote_copy(
            src_ref=src, dst_ref=dst, send_sem=ssem.at[i], recv_sem=rsem.at[i],
            device_id=dev, device_id_type=MESH,
        )

    def send(key, src, dst, dev):
        copy = remote(key, src, dst, dev)
        copy.start()
        pending.append(copy)

    def arrived(key, dst, dev):
        remote(key, dst, dst, dev).wait_recv()

    def here(src, dst):
        copy = pltpu.make_async_copy(src, dst, lsem.at[len(local)])
        copy.start()
        local.append(copy)
        return copy

    def rows_of(j):
        return pl.ds(pl.multiple_of(j * V, V), V)

    def cols_of(j):
        return pl.ds(pl.multiple_of(j * GC, GC), GC)

    def head_cols(j, h):
        return pl.ds(pl.multiple_of(j * GC + h * HD, HD), HD)

    peers = [sdev(d) for d in (1, 2, 3)] + [xsdev(d) for d in range(NS)]
    peers += [ydev(k) for k in range(1, NY)] + [zdev(k) for k in range(1, NZ)]
    barrier = pltpu.get_barrier_semaphore()
    for dev in peers:
        pl.semaphore_signal(barrier, inc=1, device_id=dev, device_id_type=MESH)

    wt[...] = jnp.zeros_like(wt)
    wt[pl.ds(0, WCOL), :] = w_own[...]
    own_w = here(wt.at[:, cols_of(s)], wslot.at[xl, s])
    own_dy = here(go, dyr.at[rows_of(s)])
    text_dy = here(tgo, dyr.at[pl.ds(VID, TXT)])
    own = []
    for src, tsrc, dst in ((vq, tq, qb), (vk, tk, kb), (vv, tv, vb)):
        own.append(here(src.at[:, cols_of(s)], dst.at[rows_of(s)]))
        own.append(here(tsrc.at[:, cols_of(s)], dst.at[pl.ds(VID, TXT)]))
    pl.semaphore_wait(barrier, len(peers))

    for d in range(NS):
        cols = wt.at[:, cols_of(seq_peer[d])]
        if d:
            send(("w", 0, d), cols, wslot.at[xl, s], sdev(d))
        send(("w", 1, d), cols, wslot.at[xl, s], xsdev(d))

    piece = V // PIECES

    def dy_piece(j, t):
        return dyr.at[pl.ds(pl.multiple_of(j * V + t * piece, piece), piece)]

    for t in range(EARLY):
        send(("dyx", t), go.at[pl.ds(t * piece, piece)], dy_piece(s, t), sdev(2))

    def send_in(h):
        for d in (2, 3, 1):
            for n, (src, dst) in enumerate(((vq, qb), (vk, kb), (vv, vb))):
                send(("in", h, d, n), src.at[:, head_cols(seq_peer[d], h)],
                     dst.at[rows_of(s), pl.ds(h * HD, HD)], sdev(d))

    def wait_in(h):
        for d in (2, 3, 1):
            for n, dst in enumerate((qb, kb, vb)):
                arrived(("in", h, d, n), dst.at[rows_of(seq_peer[d]), pl.ds(h * HD, HD)], sdev(d))

    own_w.wait()
    for d in range(NS):
        if d:
            arrived(("w", 0, d), wslot.at[xl, seq_peer[d]], sdev(d))
        arrived(("w", 1, d), wslot.at[1 - xl, seq_peer[d]], xsdev(d))
    for t in range(EARLY, PIECES):
        send(("dyx", t), go.at[pl.ds(t * piece, piece)], dy_piece(s, t), sdev(2))
    send("dyc", go, dyr.at[rows_of(s)], sdev(1))
    send_in(0)
    for i in range(XL):
        for j in range(NS):
            w48[i, pl.ds(j * WCOL, WCOL), :] = wslot[i, j].astype(F32)[:WCOL]
        wbuf[i, y, z] = w48[i].astype(BF)

    ca, cb = pl.ds(HD, GC - HD), pl.ds(0, HD)

    def blk_a(ky, kz):
        return wbuf.at[:, (y + NY + ky) % NY, (z + NZ + kz) % NZ, :, ca]

    def blk_b(kz):
        return wbuf.at[:, :, (z + NZ + kz) % NZ, :, cb]

    def along_y(kz):
        for k in range(1, NY):
            send(("wya", kz % NZ, k), blk_a(0, kz), blk_a(0, kz), ydev(k))

    for k in range(1, NY):
        mine = wbuf.at[:, y, z, :, cb]
        send(("wyb", k), mine, mine, ydev(k))
    send(("wza+", 0), blk_a(0, 0), blk_a(0, 0), zdev(1))
    send(("wza-", 0), blk_a(0, 0), blk_a(0, 0), zdev(-1))
    along_y(0)
    for k in range(1, NY):
        arrived(("wyb", k), wbuf.at[:, (y + NY - k) % NY, z, :, cb], ydev(-k))
    send(("wzb+", 0), blk_b(0), blk_b(0), zdev(1))
    send(("wzb-", 0), blk_b(0), blk_b(0), zdev(-1))

    def pass_on_dy(t):
        arrived(("dyx", t), dy_piece(part, t), sdev(2))
        send(("dyr", t), dy_piece(part, t), dy_piece(part, t), sdev(1))

    gate_f = gate[...].astype(F32)

    def gated(j, count):
        def body(i, carry):
            at = pl.ds(pl.multiple_of(j * V + i * 32, 32), 32)
            dyb[at, :] = (dyr[at, :].astype(F32) * gate_f).astype(BF)
            return carry
        lax.fori_loop(0, count // 32, body, 0)

    last_p, last_m = NZ // 2, NZ // 2 - 1
    for t in range(last_p):
        arrived(("wza+", t), blk_a(0, -1 - t), zdev(-1))
        if t + 1 < last_p:
            send(("wza+", t + 1), blk_a(0, -1 - t), blk_a(0, -1 - t), zdev(1))
        along_y(-1 - t)
        if t < last_m:
            arrived(("wza-", t), blk_a(0, 1 + t), zdev(1))
            if t + 1 < last_m:
                send(("wza-", t + 1), blk_a(0, 1 + t), blk_a(0, 1 + t), zdev(-1))
            along_y(1 + t)
        arrived(("wzb+", t), blk_b(-1 - t), zdev(-1))
        if t + 1 < last_p:
            send(("wzb+", t + 1), blk_b(-1 - t), blk_b(-1 - t), zdev(1))
        if t < last_m:
            arrived(("wzb-", t), blk_b(1 + t), zdev(1))
            if t + 1 < last_m:
                send(("wzb-", t + 1), blk_b(1 + t), blk_b(1 + t), zdev(-1))
        if t == 0:
            own_dy.wait()
            gated(s, V)
        if t == 1:
            text_dy.wait()
            gated(NS, TXT)
        if t == 2:
            arrived("dyc", dyr.at[rows_of(core)], sdev(1))
            gated(core, V)
            send_in(1)
    send_in(2)
    for t in range(PIECES):
        pass_on_dy(t)
    gated(part, V)

    for copy in own:
        copy.wait()
    q_gain, k_gain = qg[...], kg[...]
    gains[...] = jnp.zeros_like(gains)

    def norm(x):
        return lax.rsqrt(jnp.sum(x * x, axis=-1, keepdims=True) * (1.0 / HD) + 1e-06)

    def through_norm(x, r, u):
        return r * u - x * (r * r * r) * (jnp.sum(u * x, axis=-1, keepdims=True) * (1.0 / HD))

    def fwd(h):
        cols = pl.ds(h * HD, HD)
        qf = qb[:, cols].astype(F32)
        qn_s[h] = (qf * norm(qf) * q_gain).astype(BF)
        kf = kb[:, cols].astype(F32)
        kn = kf * norm(kf) * k_gain
        kn_s[h] = kn.astype(BF)
        knt_s[h] = kn.T.astype(BF)
        vt_s[...] = vb[:, cols].astype(F32).T.astype(BF)

        def chunk(c, carry):
            at = pl.ds(pl.multiple_of(c * QC, QC), QC)
            e = jnp.exp2(dot(kn_s[h], qn_s[h, at, :], 1, 1) * (SCALE * LOG2E))
            p = e * (1.0 / jnp.sum(e, axis=0, keepdims=True))
            p_s[h, :, at] = p
            ot_s[:, at] = dot(vt_s[...], p.astype(BF)).astype(BF)
            return carry
        lax.fori_loop(0, TOK // QC, chunk, 0)

    def bwd(h):
        cols = pl.ds(h * HD, HD)
        dk_a[...] = jnp.zeros_like(dk_a)
        dv_a[...] = jnp.zeros_like(dv_a)

        def chunk(c, carry):
            at = pl.ds(pl.multiple_of(c * QC, QC), QC)
            do = dout[at, cols]
            p = p_s[h, :, at]
            dv_a[...] += dot(p.astype(BF), do)
            dpr = dot(vb[:, cols], do, 1, 1)
            delta = jnp.sum(p * dpr, axis=0, keepdims=True)
            ds = (p * (dpr - delta)).astype(BF)
            dk_a[...] += dot(ds, qn_s[h, at, :])
            dqn = dot(knt_s[h], ds).T * SCALE
            x = qb[at, cols].astype(F32)
            r = norm(x)
            grads[h, 0, at, :] = through_norm(x, r, dqn * q_gain).astype(BF)
            gains[0:1, :] += jnp.sum(dqn * x * r, axis=0, keepdims=True)
            return carry
        lax.fori_loop(0, TOK // QC, chunk, 0)
        dkn = dk_a[...] * SCALE
        x = kb[:, cols].astype(F32)
        r = norm(x)
        grads[h, 1] = through_norm(x, r, dkn * k_gain).astype(BF)
        gains[1:2, :] += jnp.sum(dkn * x * r, axis=0, keepdims=True)
        grads[h, 2] = dv_a[...].astype(BF)

    lo, hi = pl.ds(0, HD // 2), pl.ds(HD // 2, HD // 2)

    def term(h):
        def body(i, carry):
            at = pl.ds(pl.multiple_of(i * NY * GC, NY * GC), NY * GC)
            t = dot(ot_s[...], dyb[:, at]).astype(BF)
            for j in range(NY):
                tbuf[h, i, j] = t[:, j * GC:(j + 1) * GC]
            return carry
        lax.fori_loop(0, XL, body, 0)
        far = tbuf.at[h, :, (y + 2) % NY]
        send(("ty+", h), far.at[:, lo], r1.at[h, 0], ydev(1))
        send(("ty-", h), far.at[:, hi], r1.at[h, 1], ydev(-1))

    def y_mid(h):
        for i, half, k, key in ((0, lo, 1, "+"), (1, hi, -1, "-")):
            arrived(("ty" + key, h), r1.at[h, i], ydev(-k))
            to = (y + NY + k) % NY
            for j in range(XL):
                both = tbuf[h, j, to, half].astype(F32) + r1[h, i, j].astype(F32)
                tbuf[h, j, to, half] = both.astype(BF)
            send(("tyy" + key, h), tbuf.at[h, :, to], rbuf.at[h, i], ydev(k))

    text = pl.ds(VID, TXT)
    out_local = []

    def send_out(h):
        to = head_cols(s, h)
        send(("text", h, 2), grads.at[h, :, text], o_text.at[:, :, to], sdev(2))
        for d in (2, 3):
            send(("out", h, d), grads.at[h, :, rows_of(seq_peer[d])], o_video.at[:, :, to], sdev(d))
        send(("text", h, 1), grads.at[h, :, text], o_text.at[:, :, to], sdev(1))
        send(("out", h, 1), grads.at[h, :, rows_of(seq_peer[1])], o_video.at[:, :, to], sdev(1))
        out_local.append(here(grads.at[h, :, rows_of(s)], o_video.at[:, :, to]))
        out_local.append(here(grads.at[h, :, text], o_text.at[:, :, to]))

    def y_sum(h):
        arrived(("tyy+", h), rbuf.at[h, 0], ydev(-1))
        arrived(("tyy-", h), rbuf.at[h, 1], ydev(1))
        for i in range(XL):
            total = tbuf[h, i, y].astype(F32) + rbuf[h, 0, i].astype(F32) + rbuf[h, 1, i].astype(F32)
            zs[h, :, i] = total.T.reshape(NZ, WB, HD).astype(BF)
        for k in range(1, NZ):
            send(("tz", h, k), zs.at[h, (z + k) % NZ], zr.at[h, k - 1], zdev(k))

    wait_in(0)
    fwd(0)
    for t in range(PIECES):
        arrived(("dyr", t), dy_piece(diag, t), sdev(1))
    gated(diag, V)
    term(0)
    for kz in range(NZ):
        for k in range(1, NY):
            arrived(("wya", kz, k), blk_a(-k, kz), ydev(-k))

    dout[...] = dot(dyb[...], wbuf[...].reshape(D, GC)).astype(BF)

    bwd(0)
    send_out(0)
    y_mid(0)
    wait_in(1)
    fwd(1)
    term(1)
    wait_in(2)
    fwd(2)
    term(2)
    bwd(1)
    send_out(1)
    y_mid(1)
    y_sum(0)
    bwd(2)
    send_out(2)

    g_y[y] = gains[...]
    for k in range(1, NY):
        send(("gy", k), g_y.at[y], g_y.at[y], ydev(k))

    def pass_on_text(h):
        at = o_text.at[:, :, head_cols(part, h)]
        arrived(("text", h, 2), at, sdev(2))
        send(("textr", h), at, at, sdev(1))

    def z_sum(h):
        for k in range(1, NZ):
            arrived(("tz", h, k), zr.at[h, k - 1], zdev(-k))
        total = zs[h, z].astype(F32)
        for k in range(1, NZ):
            total += zr[h, k - 1].astype(F32)
        cols = pl.ds(h * HD, HD)
        xsum[:, :, cols] = total
        send(("tx", h), xsum.at[1 - xl, :, cols], xr.at[:, cols], xdev)

    y_mid(2)
    y_sum(1)
    for k in range(1, NY):
        arrived(("gy", k), g_y.at[(y + NY - k) % NY], ydev(-k))
    g_z[z] = (g_y[0] + g_y[1]) + (g_y[2] + g_y[3])
    for k in range(1, NZ):
        send(("gz", k), g_z.at[z], g_z.at[z], zdev(k))
    z_sum(0)
    pass_on_text(0)
    y_sum(2)
    z_sum(1)
    pass_on_text(1)
    for k in range(1, NZ):
        arrived(("gz", k), g_z.at[(z + NZ - k) % NZ], zdev(-k))
    total = g_z[0]
    for k in range(1, NZ):
        total += g_z[k]
    g_x[xl, s] = total
    for d in range(NS):
        if d:
            send(("gx", 0, d), g_x.at[xl, s], g_x.at[xl, s], sdev(d))
        send(("gx", 1, d), g_x.at[xl, s], g_x.at[xl, s], xsdev(d))
    z_sum(2)
    pass_on_text(2)
    for d in range(NS):
        if d:
            arrived(("gx", 0, d), g_x.at[xl, seq_peer[d]], sdev(d))
        arrived(("gx", 1, d), g_x.at[1 - xl, seq_peer[d]], xsdev(d))
    total = g_x[0, 0]
    for j in range(1, XL * NS):
        total += g_x[j // NS, j % NS]
    o_gain[...] = total
    for h in range(G):
        arrived(("tx", h), xr.at[:, pl.ds(h * HD, HD)], xdev)
    o_w[...] = xsum[xl] + xr[...]

    for h in range(G):
        arrived(("text", h, 1), o_text.at[:, :, head_cols(core, h)], sdev(1))
        arrived(("textr", h), o_text.at[:, :, head_cols(diag, h)], sdev(1))
        for d in (1, 2, 3):
            arrived(("out", h, d), o_video.at[:, :, head_cols(seq_peer[d], h)], sdev(d))
    for copy in out_local:
        copy.wait()
    for copy in pending:
        copy.wait_send()


def place(video, text, w, gains, *rest):
    outs, (row_q, row_k, sems) = rest[:9], rest[9:]
    row_q[...] = gains[0:1, :]
    row_k[...] = gains[1:2, :]
    parts = [(text.at[n], outs[3 + n]) for n in range(3)] + [(video.at[n], outs[n]) for n in range(3)]
    parts += [(w, outs[6]), (row_q, outs[7]), (row_k, outs[8])]
    copies = [pltpu.make_async_copy(src, dst, sems.at[n]) for n, (src, dst) in enumerate(parts)]
    for copy in copies:
        copy.start()
    for copy in copies:
        copy.wait()


def shards(video_q, video_k, video_v, text_q, text_k, text_v, q_gain, k_gain, gate, out_weight, grad_out, text_grad_out):
    hbm = pl.BlockSpec(memory_space=pltpu.HBM)
    vmem = pl.BlockSpec(memory_space=pltpu.VMEM)
    video, text, w, gains = pl.pallas_call(
        kernel,
        out_shape=[
            jax.ShapeDtypeStruct((3, V, NS * GC), BF),
            jax.ShapeDtypeStruct((3, TXT, NS * GC), BF),
            jax.ShapeDtypeStruct((WB, GC), F32),
            jax.ShapeDtypeStruct((8, HD), F32),
        ],
        in_specs=[hbm] * 6 + [vmem] * 4 + [hbm] * 2,
        out_specs=[vmem] * 4,
        scratch_shapes=[
            pltpu.VMEM((16, NS * GC), BF),
            pltpu.VMEM((TOK, GC), BF),
            pltpu.VMEM((TOK, GC), BF),
            pltpu.VMEM((TOK, GC), BF),
            pltpu.VMEM((TOK, D), BF),
            pltpu.VMEM((TOK, D), BF),
            pltpu.VMEM((XL, NY, NZ, WB, GC), BF),
            pltpu.VMEM((XL, NS, 16, GC), BF),
            pltpu.VMEM((XL, WB, GC), F32),
            pltpu.VMEM((TOK, GC), BF),
            pltpu.VMEM((G, 3, TOK, HD), BF),
            pltpu.VMEM((G, TOK, TOK), F32),
            pltpu.VMEM((G, TOK, HD), BF),
            pltpu.VMEM((G, TOK, HD), BF),
            pltpu.VMEM((G, HD, TOK), BF),
            pltpu.VMEM((HD, TOK), BF),
            pltpu.VMEM((HD, TOK), BF),
            pltpu.VMEM((TOK, HD), F32),
            pltpu.VMEM((TOK, HD), F32),
            pltpu.VMEM((8, HD), F32),
            pltpu.VMEM((G, XL, NY, HD, GC), BF),
            pltpu.VMEM((G, 2, XL, HD // 2, GC), BF),
            pltpu.VMEM((G, 2, XL, HD, GC), BF),
            pltpu.VMEM((G, NZ, XL, WB, HD), BF),
            pltpu.VMEM((G, NZ - 1, XL, WB, HD), BF),
            pltpu.VMEM((XL, WB, GC), F32),
            pltpu.VMEM((WB, GC), F32),
            pltpu.VMEM((XL, NS, 8, HD), F32),
            pltpu.VMEM((NY, 8, HD), F32),
            pltpu.VMEM((NZ, 8, HD), F32),
            pltpu.SemaphoreType.DMA((SEMS,)),
            pltpu.SemaphoreType.DMA((SEMS,)),
            pltpu.SemaphoreType.DMA((16,)),
        ],
        compiler_params=pltpu.CompilerParams(
            collective_id=0, has_side_effects=True, vmem_limit_bytes=54 << 20
        ),
        cost_estimate=pl.CostEstimate(flops=7 * 10**9, bytes_accessed=14 << 20, transcendentals=1 << 21),
    )(
        video_q, video_k, video_v, text_q, text_k, text_v,
        q_gain.reshape(1, HD), k_gain.reshape(1, HD), gate, out_weight.T, grad_out, text_grad_out,
    )
    rows = [jax.ShapeDtypeStruct((V, NS * GC), BF)] * 3 + [jax.ShapeDtypeStruct((TXT, NS * GC), BF)] * 3
    outs = pl.pallas_call(
        place,
        out_shape=rows + [jax.ShapeDtypeStruct((WB, GC), F32)] + [jax.ShapeDtypeStruct((1, HD), F32)] * 2,
        in_specs=[vmem] * 4,
        out_specs=[hbm] * 9,
        scratch_shapes=[pltpu.VMEM((1, HD), F32), pltpu.VMEM((1, HD), F32), pltpu.SemaphoreType.DMA((9,))],
        cost_estimate=pl.CostEstimate(flops=0, bytes_accessed=7 << 20, transcendentals=0),
    )(video, text, w, gains)
    return (*outs[:6], outs[6].T, outs[7].reshape(HD), outs[8].reshape(HD))


def solution(mesh):
    rows, clip = P(("dp", "seq"), None), P("dp", None)
    return jax.shard_map(
        shards,
        mesh=mesh,
        in_specs=(rows,) * 3 + (clip,) * 3 + (P(), P(), clip, P(None, ("dp", "seq")), rows, clip),
        out_specs=(rows,) * 3 + (clip,) * 3 + (P("seq", "dp"), P(), P()),
        check_vma=False,
    )
```
